256 devices in a mesh: dom: 64 (over x, z, core), sub: 4 (over y).
Axes of the slice: x: 4, y: 4, z: 8, core: 2. Of those that a mesh axis runs over, the one named last changes fastest.
Arguments:
- node_features: bfloat16 [524288, 256], P(('dom', 'sub')), may hold values from -40 to 40
- cotangent: bfloat16 [524288, 256], P(('dom', 'sub')), may hold values from -23 to 23
- tile_vals: bfloat16 [16384, 128, 128], P(('dom', 'sub')), may hold values from -0.25 to 0.25
- tile_src: int32 [16384], P(('dom', 'sub')), may hold values from 0 to 21
- tile_dst: int32 [16384], P(('dom', 'sub')), may hold values from 0 to 15
- halo_rows: int32 [256, 6, 128], P(('dom', 'sub')), may hold values from 0 to 2047
- halo_count: int32 [256, 6], P(('dom', 'sub')), may hold values from 32 to 128, as said below
- w_in: bfloat16 [512, 256], replicated, may hold values from -0.25 to 0.25
- b_in: float32 [256], replicated, may hold values from -4 to 4
- w_out: bfloat16 [256, 256], replicated, may hold values from -0.375 to 0.375
Outputs:
- new_features: bfloat16 [524288, 256], P(('dom', 'sub'))
- grad_features: float32 [524288, 256], P(('dom', 'sub'))
- grad_w_in: float32 [512, 256], replicated
- grad_b_in: float32 [256], replicated
- grad_w_out: float32 [256, 256], replicated
The draws below stay inside these ranges and needn't reach their ends.
Inputs may be any that keep to these rules, and one draw needn't show every extreme that they name: `halo_count`: one device, drawn from the seed, has 128 live rows in every slot.
All inputs are finite; a program needn't handle non-finite values.
Results may differ from the reference program's by a relative error of at most 0.0075.
Values may be sent and summed in bfloat16 or wider, within the bound.
No kernel may reach another device: no remote copies, remote signals or barrier semaphores. Data moves between devices by JAX's collectives and lax.ppermute only.
A program may use at most 128 MiB of HBM per device.

```python
import jax
import jax.numpy as jnp
from jax import lax

H = 256
BLK = 128
NB = 16
TPB = 4
HR = 128
NODE_DEV = 2048
TILES_DEV = 64
PEERS = 6
BUF_BLOCKS = 22
NODES = 524288
TILES = 16384
N_DOM = 64
N_SUB = 4
DEVICES = 256


def draw_node_features(key, part):
    key = jax.random.fold_in(key, 11)
    key_base, key_rows, key_cols = jax.random.split(key, 3)
    row_scale = jnp.power(10.0, jax.random.uniform(key_rows, (NODES, 1), minval=-0.5, maxval=0.5))
    col_scale = jnp.power(10.0, jax.random.uniform(key_cols, (1, H), minval=-0.5, maxval=0.5))
    base_draw = jax.random.truncated_normal(key_base, -4.0, 4.0, (NODES, H))
    return (base_draw * row_scale * col_scale).astype(jnp.bfloat16)


def draw_cotangent(key, part):
    key = jax.random.fold_in(key, 23)
    key_base, key_rows = jax.random.split(key, 2)
    position = jnp.arange(NODES, dtype=jnp.float32)[:, None] / NODES
    row_scale = jnp.power(10.0, jax.random.uniform(key_rows, (NODES, 1), minval=-0.5, maxval=0.5))
    row_scale = row_scale * jnp.power(3.0, position) / 1.7
    base_draw = jax.random.truncated_normal(key_base, -4.0, 4.0, (NODES, H))
    return (base_draw * row_scale).astype(jnp.bfloat16)


def draw_halo_count(key, part):
    key = jax.random.fold_in(key, 37)
    key_counts, key_device = jax.random.split(key, 2)
    counts = jax.random.randint(key_counts, (DEVICES, PEERS), HR // 4, HR + 1)
    chosen = jax.random.randint(key_device, (), 0, DEVICES)
    device_ids = jnp.arange(DEVICES, dtype=jnp.int32)[:, None]
    return jnp.where(device_ids == chosen, HR, counts).astype(jnp.int32)


def plant(drawn, key, least, high):
    spot = [jax.random.randint(jax.random.fold_in(key, axis), (), 0, length) for axis, length in enumerate(drawn.shape)]
    main_axis = drawn.shape.index(max(drawn.shape))
    beside = spot[:main_axis] + [(spot[main_axis] + 1) % drawn.shape[main_axis]] + spot[main_axis + 1:]
    return drawn.at[tuple(spot)].set(least).at[tuple(beside)].set(high)


def block_levels(stream_key, dims, pieces, least, largest):
    loudness, own = 1.0, jax.random.fold_in(stream_key, 6)
    for axis_at, blocks in pieces:
        draws = jnp.exp(jax.random.uniform(jax.random.fold_in(own, axis_at), (blocks,), jnp.float32, least / len(pieces), largest / len(pieces)))
        loudness = loudness * jnp.repeat(draws, dims[axis_at] // blocks).reshape([-1 if axis == axis_at else 1 for axis in range(len(dims))])
    return loudness


def scatter_about(key, dims, deviation, reach, cuts=(), kind=jnp.bfloat16):
    entries = deviation * jax.random.normal(key, dims, jnp.float32)
    if cuts:
        entries = entries * block_levels(key, dims, cuts, -0.22, 0.18)
    return jnp.clip(entries, -reach, reach).astype(kind)


def setup_inputs(seed: int = 0) -> dict:
    key_of = jax.random.split(jax.random.key(seed), 11)
    return {
        "node_features": draw_node_features(jax.random.fold_in(key_of[10], 71), 0),
        "cotangent": draw_cotangent(jax.random.fold_in(key_of[10], 71), 0),
        "tile_vals": scatter_about(key_of[2], (TILES, BLK, BLK), (BLK * TPB) ** -0.5, 0.25, ((0, 256),)),
        "tile_src": plant(jax.random.randint(key_of[3], (TILES,), 0, BUF_BLOCKS), jax.random.fold_in(key_of[3], 1), 0, BUF_BLOCKS - 1).astype(jnp.int32),
        "tile_dst": plant(jax.random.randint(key_of[4], (TILES,), 0, NB), jax.random.fold_in(key_of[4], 1), 0, NB - 1).astype(jnp.int32),
        "halo_rows": plant(jax.random.randint(key_of[5], (DEVICES, PEERS, HR), 0, NODE_DEV), jax.random.fold_in(key_of[5], 1), 0, NODE_DEV - 1).astype(jnp.int32),
        "halo_count": draw_halo_count(jax.random.fold_in(key_of[10], 71), 0),
        "w_in": scatter_about(key_of[7], (2 * H, H), (2 * H) ** -0.5, 0.25),
        "b_in": scatter_about(key_of[8], (H,), 1.0, 4.0, (), jnp.float32),
        "w_out": scatter_about(key_of[9], (H, H), H ** -0.5, 0.375),
    }


clip_norm = 256.0
ln_eps = 1e-05

def silu_slope(preact):
    sigmoid_v = jax.nn.sigmoid(preact)
    return sigmoid_v * (1.0 + preact * (1.0 - sigmoid_v))

def node_update(feature_rows, aggregate, w_in, b_in, w_out, cotangent):
    joined = jnp.concatenate([feature_rows, aggregate], axis=1)
    preact = jnp.dot(joined, w_in, preferred_element_type=jnp.float32) + b_in
    activated = jax.nn.silu(preact).astype(jnp.bfloat16)
    lifted = jnp.dot(activated, w_out, preferred_element_type=jnp.float32)
    centred = lifted - lax.optimization_barrier(jnp.mean(lifted, axis=1, keepdims=True))
    inv_std = lax.rsqrt(lax.optimization_barrier(jnp.mean(centred * centred, axis=1, keepdims=True)) + ln_eps)
    normed = centred * inv_std
    new_rows = (feature_rows.astype(jnp.float32) + normed).astype(jnp.bfloat16)
    upstream = cotangent.astype(jnp.float32)
    grad_lifted = inv_std * (upstream - lax.optimization_barrier(jnp.mean(upstream, axis=1, keepdims=True)) - normed * lax.optimization_barrier(jnp.mean(upstream * normed, axis=1, keepdims=True)))
    grad_lifted = grad_lifted.astype(jnp.bfloat16)
    grad_out = jnp.dot(activated.T, grad_lifted, preferred_element_type=jnp.float32)
    grad_act = jnp.dot(grad_lifted, w_out.T, preferred_element_type=jnp.float32)
    grad_pre = (grad_act * silu_slope(preact)).astype(jnp.bfloat16)
    grad_in = jnp.dot(joined.T, grad_pre, preferred_element_type=jnp.float32)
    grad_bias = lax.optimization_barrier(jnp.sum(grad_pre.astype(jnp.float32), axis=0))
    grad_joined = jnp.dot(grad_pre, w_in.T, preferred_element_type=jnp.float32)
    latent = feature_rows.shape[1]
    direct = upstream + grad_joined[:, :latent]
    grad_agg = grad_joined[:, latent:].astype(jnp.bfloat16)
    return (new_rows, direct, grad_agg, grad_in, grad_bias, grad_out)

def pick_rows(local_rows, row_ids):
    return local_rows[row_ids]

def add_back(row_ids, values):
    return jnp.zeros((NB * BLK, H), jnp.float32).at[row_ids.reshape(-1)].add(values.reshape(-1, H))

def reference(node_features, cotangent, tile_vals, tile_src, tile_dst, halo_rows, halo_count, w_in, b_in, w_out):
    device_count = N_DOM * N_SUB
    node_count = NB * BLK
    features = node_features.reshape(device_count, node_count, H)
    live_mask = jnp.arange(HR, dtype=jnp.int32)[None, None, :] < halo_count[:, :, None]
    picked = jax.vmap(pick_rows)(features, halo_rows)
    outgoing = jnp.where(live_mask[..., None], picked, jnp.zeros_like(picked))
    outgoing = outgoing.reshape(N_DOM, N_SUB, PEERS, HR, H)
    from_sub = jnp.swapaxes(outgoing[:, :, :N_SUB], 1, 2)
    from_left = jnp.roll(outgoing[:, :, N_SUB], 1, axis=0)
    from_right = jnp.roll(outgoing[:, :, N_SUB + 1], -1, axis=0)
    halo_part = jnp.concatenate([from_sub, from_left[:, :, None], from_right[:, :, None]], axis=2)
    buffers = jnp.concatenate([features, halo_part.reshape(device_count, PEERS * HR, H)], axis=1)
    tile_blocks = tile_vals.reshape(device_count, TILES_DEV, BLK, BLK)
    sources = tile_src.reshape(device_count, TILES_DEV)
    targets = tile_dst.reshape(device_count, TILES_DEV)
    upstreams = cotangent.reshape(device_count, node_count, H)

    def one_device(operands):
        buffer, tiles, source_ids, target_ids, feature_rows, upstream = operands
        gathered = buffer.reshape(-1, BLK, H)[source_ids]
        products = jnp.einsum('tij,tjh->tih', tiles.astype(jnp.float32), gathered.astype(jnp.float32))
        aggregate = jax.ops.segment_sum(products, target_ids, num_segments=NB)
        aggregate = aggregate.reshape(node_count, H).astype(jnp.bfloat16)
        new_rows, direct, grad_agg, grad_in, grad_bias, grad_out = node_update(feature_rows, aggregate, w_in, b_in, w_out, upstream)
        down_blocks = grad_agg.reshape(NB, BLK, H)[target_ids]
        backward = jnp.einsum('tji,tjh->tih', tiles.astype(jnp.float32), down_blocks.astype(jnp.float32))
        grad_buffer = jax.ops.segment_sum(backward, source_ids, num_segments=BUF_BLOCKS).reshape(-1, H)
        return (new_rows, direct + grad_buffer[:node_count], grad_buffer[node_count:], grad_in, grad_bias, grad_out)
    new_rows, grad_local, halo_grad, grad_in, grad_bias, grad_out = lax.map(one_device, (buffers, tile_blocks, sources, targets, features, upstreams))
    halo_grad = halo_grad.reshape(N_DOM, N_SUB, PEERS, HR, H)
    back_sub = jnp.swapaxes(halo_grad[:, :, :N_SUB], 1, 2)
    back_left = jnp.roll(halo_grad[:, :, N_SUB], -1, axis=0)
    back_right = jnp.roll(halo_grad[:, :, N_SUB + 1], 1, axis=0)
    returned = jnp.concatenate([back_sub, back_left[:, :, None], back_right[:, :, None]], axis=2)
    returned = returned.reshape(device_count, PEERS, HR, H)
    returned = jnp.where(live_mask[..., None], returned, jnp.zeros_like(returned))
    grad_features = grad_local + jax.vmap(add_back)(halo_rows, returned)
    sum_in = lax.optimization_barrier(jnp.sum(grad_in, axis=0))
    sum_bias = lax.optimization_barrier(jnp.sum(grad_bias, axis=0))
    sum_out = lax.optimization_barrier(jnp.sum(grad_out, axis=0))
    squares = jnp.sum(sum_in * sum_in) + jnp.sum(sum_bias * sum_bias) + jnp.sum(sum_out * sum_out)
    factor = jnp.minimum(1.0, clip_norm / jnp.sqrt(squares + 1e-06))
    return (new_rows.reshape(NODES, H), grad_features.reshape(NODES, H), sum_in * factor, sum_bias * factor, sum_out * factor)
```

```python
import jax
import jax.numpy as jnp
from jax import lax
from jax.experimental import pallas as pl
from jax.experimental.pallas import tpu as pltpu
from jax.sharding import Mesh, PartitionSpec as P

H = 256
BLK = 128
NB = 16
N = NB * BLK
T = 64
PEERS = 6
SUB = 4
BUF = NB + PEERS
CHUNKS = 16
CROWS = 56
CH = 256
UNROLL = 4
clip_norm = 256.0
ln_eps = 1e-05
F32 = jnp.float32
BF16 = jnp.bfloat16
ALL = ("x", "z", "core", "sub")
DOM = ("x", "z", "core")
PLANE = ("x", "sub")
MIB = 1024 * 1024
VM = pl.BlockSpec(memory_space=pltpu.VMEM)
SM = pl.BlockSpec(memory_space=pltpu.SMEM)


def params(mib):
    return pltpu.CompilerParams(vmem_limit_bytes=mib * MIB)


def sds(shape, dtype):
    return jax.ShapeDtypeStruct(shape, dtype)


def dot(a, b):
    return jnp.dot(a, b, preferred_element_type=F32)


def dot_t0(a, b):
    return lax.dot_general(a, b, (((0,), (0,)), ((), ())), preferred_element_type=F32)


def dot_t1(a, b):
    return lax.dot_general(a, b, (((1,), (1,)), ((), ())), preferred_element_type=F32)


def pick_kernel(rows_ref, count_ref, feat_ref, *outs):
    me = lax.axis_index("sub")
    for d in range(PEERS):
        q = lax.rem(me + d, SUB) if d < SUB else d
        ids = rows_ref[0, pl.ds(q, 1), :]
        lane = lax.broadcasted_iota(jnp.int32, (1, BLK), 1)
        ids = jnp.where(lane < count_ref[0, q], ids, -1)
        column = jnp.transpose(jnp.broadcast_to(ids, (8, BLK)))[:, :1]
        hot = lax.broadcasted_iota(jnp.int32, (BLK, N), 1) == column
        hot = jnp.where(hot, 1.0, 0.0).astype(BF16)
        outs[d][...] = dot(hot, feat_ref[...]).astype(BF16)


def list_tiles(src_ref, dst_ref, listed, least, most):
    def step(t, n):
        s = src_ref[t]
        listed[n] = (dst_ref[t] * 32 + s) * 64 + t
        return n + jnp.where((s >= least) & (s < most), 1, 0)

    n = lax.fori_loop(0, T, step, jnp.int32(0))
    for p in range(UNROLL):
        listed[n + p] = (NB * 32 + least) * 64
    return n


def near_kernel(src_ref, dst_ref, feat_ref, vals_ref, total, listed):
    n = list_tiles(src_ref, dst_ref, listed, 0, NB)
    total[...] = jnp.zeros_like(total)

    def step(i, _):
        for u in range(UNROLL):
            packed = listed[i * UNROLL + u]
            t, s, d = packed % 64, (packed // 64) % 32, packed // 2048
            rows = feat_ref[pl.ds(pl.multiple_of(s * BLK, BLK), BLK), :]
            total[d] += dot(vals_ref[t], rows)
        return 0

    lax.fori_loop(0, pl.cdiv(n, UNROLL), step, 0)


def node_kernel(
    src_ref, dst_ref, h0, h1, h2, h3, h4, h5, feat_ref, cot_ref, vals_ref, near_ref,
    win_ref, bin_ref, wout_ref, new_ref, gpre_ref, pay_ref, listed, halo, total, sum_in, sum_out, sem,
):
    copy = pltpu.make_async_copy(near_ref, total, sem)
    copy.start()
    n = list_tiles(src_ref, dst_ref, listed, NB, BUF)
    me = lax.axis_index("sub")
    for d, h in enumerate((h0, h1, h2, h3, h4, h5)):
        q = lax.rem(me + SUB - d, SUB) if d < SUB else d
        halo[q] = h[...]
    copy.wait()

    def step(i, _):
        for u in range(UNROLL):
            packed = listed[i * UNROLL + u]
            t, s, d = packed % 64, (packed // 64) % 32, packed // 2048
            total[d] += dot(vals_ref[t], halo[s - NB])
        return 0

    lax.fori_loop(0, pl.cdiv(n, UNROLL), step, 0)
    w_in, b_in, w_out = win_ref[...], bin_ref[...], wout_ref[...]
    sum_bias = jnp.zeros((1, H), F32)
    for c in range(N // CH):
        rows = pl.ds(c * CH, CH)
        per = CH // BLK
        agg = total[pl.ds(c * per, per)].reshape(CH, H).astype(BF16)
        feat = feat_ref[rows, :]
        joined = jnp.concatenate([feat, agg], axis=1)
        pre = dot(joined, w_in) + b_in
        sig = 1.0 / (1.0 + jnp.exp(-pre))
        act = (pre * sig).astype(BF16)
        slope = sig * (1.0 + pre * (1.0 - sig))
        lifted = dot(act, w_out)
        centred = lifted - jnp.mean(lifted, axis=1, keepdims=True)
        inv_std = lax.rsqrt(jnp.mean(centred * centred, axis=1, keepdims=True) + ln_eps)
        normed = centred * inv_std
        new_ref[rows, :] = (feat.astype(F32) + normed).astype(BF16)
        up = cot_ref[rows, :].astype(F32)
        grad_lifted = inv_std * (
            up
            - jnp.mean(up, axis=1, keepdims=True)
            - normed * jnp.mean(up * normed, axis=1, keepdims=True)
        )
        grad_lifted = grad_lifted.astype(BF16)
        gpre = (dot_t1(grad_lifted, w_out) * slope).astype(BF16)
        gpre_ref[rows, :] = gpre
        g_out = dot_t0(act, grad_lifted)
        g_in = dot_t0(joined, gpre)
        sum_bias = sum_bias + jnp.sum(gpre.astype(F32), axis=0, keepdims=True)
        if c == 0:
            sum_in[...] = g_in
            sum_out[...] = g_out
        else:
            sum_in[...] += g_in
            sum_out[...] += g_out
    for k in range(CHUNKS):
        last = jnp.broadcast_to(sum_bias, (8, H)) if k == 0 else jnp.zeros((8, H), F32)
        piece = jnp.concatenate(
            [sum_in[pl.ds(32 * k, 32), :], sum_out[pl.ds(16 * k, 16), :], last], axis=0
        )
        pay_ref[k] = piece.astype(BF16)


def back_kernel(
    src_ref, dst_ref, gpre_ref, cot_ref, vals_ref, win_ref, own_ref, o0, o1, o2, o3, o4, o5, grad_agg, total
):
    w_in = win_ref[...]
    for c in range(N // CH):
        rows = pl.ds(c * CH, CH)
        per = CH // BLK
        joined = dot_t1(gpre_ref[rows, :], w_in)
        grad_agg[rows, :] = joined[:, H:].astype(BF16)
        direct = cot_ref[rows, :].astype(F32) + joined[:, :H]
        total[pl.ds(c * per, per)] = direct.reshape(per, BLK, H)
    total[pl.ds(NB, PEERS)] = jnp.zeros((PEERS, BLK, H), F32)

    def step(i, _):
        for u in range(UNROLL):
            t = i * UNROLL + u
            s, d = src_ref[t], dst_ref[t]
            down = grad_agg[pl.ds(pl.multiple_of(d * BLK, BLK), BLK), :]
            total[s] += dot_t0(vals_ref[t], down)
        return 0

    lax.fori_loop(0, T // UNROLL, step, 0)
    own_ref[...] = total[pl.ds(0, NB)].reshape(N, H)
    me = lax.axis_index("sub")
    for d, o in enumerate((o0, o1, o2, o3, o4, o5)):
        q = lax.rem(me + d, SUB) if d < SUB else d
        o[...] = total[NB + q].astype(BF16)


def land_kernel(rows_ref, count_ref, r0, r1, r2, r3, r4, r5, own_ref, out_ref):
    me = lax.axis_index("sub")
    lane = lax.broadcasted_iota(jnp.int32, (1, BLK), 1)
    ids = []
    for d in range(PEERS):
        q = lax.rem(me + SUB - d, SUB) if d < SUB else d
        ids.append(jnp.where(lane < count_ref[0, q], rows_ref[0, pl.ds(q, 1), :], -1))
    ids = jnp.concatenate(ids, axis=1)
    back = jnp.concatenate([r[...] for r in (r0, r1, r2, r3, r4, r5)], axis=0)
    for c in range(N // CH):
        rows = pl.ds(c * CH, CH)
        hot = lax.broadcasted_iota(jnp.int32, (CH, PEERS * BLK), 0) + c * CH == ids
        hot = jnp.where(hot, 1.0, 0.0).astype(BF16)
        out_ref[rows, :] = own_ref[rows, :] + dot(hot, back)


def fold_kernel(parts, out_ref):
    out_ref[...] = jnp.sum(parts[...].astype(F32), axis=0).astype(BF16)


def pair_kernel(mine, other, out_ref):
    both = (mine[...].astype(F32) + other[...].astype(F32)).astype(BF16)
    for i in range(out_ref.shape[0]):
        out_ref[i] = both


def spread_kernel(parts, out_ref):
    whole = jnp.sum(parts[...].astype(F32), axis=0).astype(BF16)
    for i in range(out_ref.shape[0]):
        out_ref[i] = whole


def clip_kernel(parts, in_ref, bias_ref, out_ref):
    squares = jnp.zeros((8, H), F32)
    for k in range(CHUNKS):
        piece = parts[k].astype(F32)
        squares = squares + jnp.sum(jnp.square(piece[:48]).reshape(6, 8, H), axis=0)
    bias = parts[0].astype(F32)[48:49]
    norm = jnp.sum(squares, keepdims=True) + jnp.sum(jnp.square(bias), keepdims=True)
    factor = jnp.minimum(1.0, clip_norm * lax.rsqrt(norm + 1e-06))
    for k in range(CHUNKS):
        piece = parts[k].astype(F32) * factor
        in_ref[pl.ds(32 * k, 32), :] = piece[:32]
        out_ref[pl.ds(16 * k, 16), :] = piece[32:48]
    bias_ref[...] = bias * factor


def shift(value, axis, by, size):
    return lax.ppermute(value, axis, [(i, (i + by) % size) for i in range(size)])


def exchange(slots):
    got = [slots[0]]
    got += [shift(slots[d], "sub", d, SUB) for d in range(1, SUB)]
    dom = 1
    for axis in DOM:
        dom *= lax.axis_size(axis)
    return got, dom


def local(feat, cot, vals, src, dst, halo_rows, halo_count, w_in, b_in, w_out):
    block = sds((BLK, H), BF16)
    slots = pl.pallas_call(
        pick_kernel,
        out_shape=[block] * PEERS,
        in_specs=[VM, SM, VM],
        out_specs=[VM] * PEERS,
        compiler_params=params(24),
        name="pick",
    )(halo_rows, halo_count, feat)
    got, dom = exchange(slots)
    got += [shift(slots[4], DOM, 1, dom), shift(slots[5], DOM, -1, dom)]
    near = pl.pallas_call(
        near_kernel,
        out_shape=sds((NB + 1, BLK, H), F32),
        in_specs=[SM, SM, VM, VM],
        out_specs=VM,
        scratch_shapes=[pltpu.SMEM((T + UNROLL,), jnp.int32)],
        compiler_params=params(24),
        cost_estimate=pl.CostEstimate(flops=800_000_000, bytes_accessed=6_000_000, transcendentals=0),
        name="near",
    )(src, dst, feat, vals)
    new_rows, gpre, pay = pl.pallas_call(
        node_kernel,
        out_shape=[sds((N, H), BF16), sds((N, H), BF16), sds((CHUNKS, CROWS, H), BF16)],
        in_specs=[SM, SM] + [VM] * 9 + [pl.BlockSpec(memory_space=pl.ANY)] + [VM] * 3,
        out_specs=[VM] * 3,
        scratch_shapes=[
            pltpu.SMEM((T + UNROLL,), jnp.int32),
            pltpu.VMEM((PEERS, BLK, H), BF16),
            pltpu.VMEM((NB + 1, BLK, H), F32),
            pltpu.VMEM((2 * H, H), F32),
            pltpu.VMEM((H, H), F32),
            pltpu.SemaphoreType.DMA,
        ],
        compiler_params=params(32),
        name="node",
    )(src, dst, *got, feat, cot, vals, near, w_in, b_in.reshape(1, H), w_out)
    parts = lax.all_to_all(pay, PLANE, split_axis=0, concat_axis=0, tiled=True)
    back = pl.pallas_call(
        back_kernel,
        out_shape=[sds((N, H), F32)] + [block] * PEERS,
        in_specs=[SM, SM] + [VM] * 4,
        out_specs=[VM] * 7,
        scratch_shapes=[pltpu.VMEM((N, H), BF16), pltpu.VMEM((BUF, BLK, H), F32)],
        compiler_params=params(32),
        cost_estimate=pl.CostEstimate(flops=4_000_000_000, bytes_accessed=9_000_000, transcendentals=0),
        name="back",
    )(src, dst, gpre, cot, vals, w_in)
    own, slots = back[0], back[1:]
    got, dom = exchange(slots)
    got += [shift(slots[4], DOM, -1, dom), shift(slots[5], DOM, 1, dom)]
    grad_features = pl.pallas_call(
        land_kernel,
        out_shape=sds((N, H), F32),
        in_specs=[VM, SM] + [VM] * 7,
        out_specs=VM,
        compiler_params=params(24),
        cost_estimate=pl.CostEstimate(flops=3_000_000_000, bytes_accessed=5_000_000, transcendentals=0),
        name="land",
    )(halo_rows, halo_count, *got, own)
    piece = sds((CROWS, H), BF16)
    folded = pl.pallas_call(
        fold_kernel, out_shape=piece, in_specs=[VM], out_specs=VM, compiler_params=params(4), name="fold"
    )(parts)
    other = shift(folded, "core", 1, 2)
    depth = lax.axis_size("z")
    paired = pl.pallas_call(
        pair_kernel,
        out_shape=sds((depth, CROWS, H), BF16),
        in_specs=[VM] * 2,
        out_specs=VM,
        compiler_params=params(4),
        name="pair",
    )(folded, other)
    column = lax.all_to_all(paired, "z", split_axis=0, concat_axis=0, tiled=True)
    spread = pl.pallas_call(
        spread_kernel,
        out_shape=sds((CHUNKS, CROWS, H), BF16),
        in_specs=[VM],
        out_specs=VM,
        compiler_params=params(4),
        name="spread",
    )(column)
    whole = lax.all_to_all(spread, PLANE, split_axis=0, concat_axis=0, tiled=True)
    g_in, g_bias, g_out = pl.pallas_call(
        clip_kernel,
        out_shape=[sds((2 * H, H), F32), sds((1, H), F32), sds((H, H), F32)],
        in_specs=[VM],
        out_specs=[VM] * 3,
        compiler_params=params(8),
        name="clip",
    )(whole)
    return new_rows, grad_features, g_in, g_bias.reshape(H), g_out


def solution(mesh):
    grid = Mesh(mesh.devices.reshape(4, 8, 2, 4), ALL)
    split2, split1 = P(ALL, None), P(ALL)
    split3 = P(ALL, None, None)
    return jax.shard_map(
        local,
        mesh=grid,
        in_specs=(split2, split2, split3, split1, split1, split3, split2, P(), P(), P()),
        out_specs=(split2, split2, P(), P(), P()),
        check_vma=False,
    )
```

```python
import jax
import jax.numpy as jnp
from jax import lax
from jax.experimental import pallas as pl
from jax.experimental.pallas import tpu as pltpu
from jax.sharding import Mesh, PartitionSpec as P

H = 256
BLK = 128
NB = 16
N = NB * BLK
T = 64
PEERS = 6
SUB = 4
BUF = NB + PEERS
CHUNKS = 16
CROWS = 56
CH = 1024
NEAR_STEP = 16
FAR_STEP = 8
BACK_STEP = 64
clip_norm = 256.0
ln_eps = 1e-05
F32 = jnp.float32
BF16 = jnp.bfloat16
ALL = ("x", "z", "core", "sub")
DOM = ("x", "z", "core")
PLANE = ("x", "sub")
MIB = 1024 * 1024
VM = pl.BlockSpec(memory_space=pltpu.VMEM)
HB = pl.BlockSpec(memory_space=pltpu.HBM)
SM = pl.BlockSpec(memory_space=pltpu.SMEM)


def params(mib):
    return pltpu.CompilerParams(vmem_limit_bytes=mib * MIB)


def sds(shape, dtype):
    return jax.ShapeDtypeStruct(shape, dtype)


def dot(a, b):
    return jnp.dot(a, b, preferred_element_type=F32)


def dot_t0(a, b):
    return lax.dot_general(a, b, (((0,), (0,)), ((), ())), preferred_element_type=F32)


def dot_t1(a, b):
    return lax.dot_general(a, b, (((1,), (1,)), ((), ())), preferred_element_type=F32)


def pick_kernel(rows_hbm, count_hbm, feat_hbm, o0, o1, o2, o3, o4, o5, rows, count, feat, hot, sems):
    load_rows = pltpu.make_async_copy(rows_hbm, rows, sems.at[0])
    load_count = pltpu.make_async_copy(count_hbm, count, sems.at[1])
    load_feat = pltpu.make_async_copy(feat_hbm, feat, sems.at[2])
    load_rows.start()
    load_count.start()
    load_feat.start()
    me = lax.axis_index("sub")
    load_rows.wait()
    load_count.wait()
    lane = lax.broadcasted_iota(jnp.int32, (1, BLK), 1)
    node = lax.broadcasted_iota(jnp.int32, (BLK, N), 1)
    for d in range(PEERS):
        q = lax.rem(me + d, SUB) if d < SUB else d
        ids = jnp.where(lane < count[0, q], rows[q], -1)
        column = jnp.transpose(jnp.broadcast_to(ids, (8, BLK)))[:, :1]
        hot[pl.ds(d * BLK, BLK), :] = jnp.where(node == column, 1.0, 0.0).astype(BF16)
    load_feat.wait()
    picked = dot(hot[...], feat[...]).astype(BF16)
    for d, o in enumerate((o0, o1, o2, o3, o4, o5)):
        o[...] = picked[d * BLK : (d + 1) * BLK]


def list_tiles(src_ref, dst_ref, listed, least, most, spare):
    def step(t, n):
        s = src_ref[t]
        listed[n] = (dst_ref[t] * 32 + s) * 64 + t
        return n + jnp.where((s >= least) & (s < most), 1, 0)

    n = lax.fori_loop(0, T, step, jnp.int32(0), unroll=True)
    for p in range(spare):
        listed[n + p] = (NB * 32 + least) * 64
    return n


def near_kernel(src_hbm, dst_hbm, feat_hbm, vals_hbm, total, src, dst, listed, feat, vals, sems):
    load_src = pltpu.make_async_copy(src_hbm, src, sems.at[0])
    load_dst = pltpu.make_async_copy(dst_hbm, dst, sems.at[1])
    load_feat = pltpu.make_async_copy(feat_hbm, feat, sems.at[2])
    load_vals = pltpu.make_async_copy(vals_hbm, vals, sems.at[3])
    load_src.start()
    load_dst.start()
    load_feat.start()
    load_vals.start()
    total[...] = jnp.zeros_like(total)
    load_src.wait()
    load_dst.wait()
    n = list_tiles(src, dst, listed, 0, NB, NEAR_STEP)
    load_feat.wait()
    load_vals.wait()

    def step(i, _):
        for u in range(NEAR_STEP):
            packed = listed[i * NEAR_STEP + u]
            t, s, d = packed % 64, (packed // 64) % 32, packed // 2048
            rows = feat[pl.ds(pl.multiple_of(s * BLK, BLK), BLK), :]
            total[d] += dot(vals[t], rows)
        return 0

    lax.fori_loop(0, pl.cdiv(n, NEAR_STEP), step, 0)


def node_kernel(
    src_ref, dst_ref, h0, h1, h2, h3, h4, h5, feat_ref, cot_ref, vals_ref, near_ref,
    win_ref, bin_ref, wout_ref, new_ref, gpre_ref, pay_ref, listed, halo, total, sum_in, sum_out,
):
    n = list_tiles(src_ref, dst_ref, listed, NB, BUF, FAR_STEP)
    me = lax.axis_index("sub")
    for d, h in enumerate((h0, h1, h2, h3, h4, h5)):
        q = lax.rem(me + SUB - d, SUB) if d < SUB else d
        halo[q] = h[...]
    total[...] = near_ref[...]

    def step(i, _):
        for u in range(FAR_STEP):
            packed = listed[i * FAR_STEP + u]
            t, s, d = packed % 64, (packed // 64) % 32, packed // 2048
            total[d] += dot(vals_ref[t], halo[s - NB])
        return 0

    lax.fori_loop(0, pl.cdiv(n, FAR_STEP), step, 0)
    w_in, b_in, w_out = win_ref[...], bin_ref[...], wout_ref[...]
    sum_bias = jnp.zeros((1, H), F32)
    for c in range(N // CH):
        rows = pl.ds(c * CH, CH)
        per = CH // BLK
        agg = total[pl.ds(c * per, per)].reshape(CH, H).astype(BF16)
        feat = feat_ref[rows, :]
        joined = jnp.concatenate([feat, agg], axis=1)
        pre = dot(joined, w_in) + b_in
        sig = 1.0 / (1.0 + jnp.exp(-pre))
        act = (pre * sig).astype(BF16)
        slope = sig * (1.0 + pre * (1.0 - sig))
        lifted = dot(act, w_out)
        centred = lifted - jnp.mean(lifted, axis=1, keepdims=True)
        inv_std = lax.rsqrt(jnp.mean(centred * centred, axis=1, keepdims=True) + ln_eps)
        normed = centred * inv_std
        new_ref[rows, :] = (feat.astype(F32) + normed).astype(BF16)
        up = cot_ref[rows, :].astype(F32)
        grad_lifted = inv_std * (
            up
            - jnp.mean(up, axis=1, keepdims=True)
            - normed * jnp.mean(up * normed, axis=1, keepdims=True)
        )
        grad_lifted = grad_lifted.astype(BF16)
        gpre = (dot_t1(grad_lifted, w_out) * slope).astype(BF16)
        gpre_ref[rows, :] = gpre
        g_out = dot_t0(act, grad_lifted)
        g_in = dot_t0(joined, gpre)
        sum_bias = sum_bias + jnp.sum(gpre.astype(F32), axis=0, keepdims=True)
        if c == 0:
            sum_in[...] = g_in
            sum_out[...] = g_out
        else:
            sum_in[...] += g_in
            sum_out[...] += g_out
    for k in range(CHUNKS):
        last = jnp.broadcast_to(sum_bias, (8, H)) if k == 0 else jnp.zeros((8, H), F32)
        piece = jnp.concatenate(
            [sum_in[pl.ds(32 * k, 32), :], sum_out[pl.ds(16 * k, 16), :], last], axis=0
        )
        pay_ref[k] = piece.astype(BF16)


def back_kernel(
    src_ref, dst_ref, gpre_ref, cot_ref, vals_ref, win_ref, own_ref, o0, o1, o2, o3, o4, o5, grad_agg, total
):
    w_in = win_ref[...]
    for c in range(N // CH):
        rows = pl.ds(c * CH, CH)
        per = CH // BLK
        joined = dot_t1(gpre_ref[rows, :], w_in)
        grad_agg[rows, :] = joined[:, H:].astype(BF16)
        direct = cot_ref[rows, :].astype(F32) + joined[:, :H]
        total[pl.ds(c * per, per)] = direct.reshape(per, BLK, H)
    total[pl.ds(NB, PEERS)] = jnp.zeros((PEERS, BLK, H), F32)

    def step(i, _):
        for u in range(BACK_STEP):
            t = i * BACK_STEP + u
            s, d = src_ref[t], dst_ref[t]
            down = grad_agg[pl.ds(pl.multiple_of(d * BLK, BLK), BLK), :]
            total[s] += dot_t0(vals_ref[t], down)
        return 0

    lax.fori_loop(0, T // BACK_STEP, step, 0)
    own_ref[...] = total[pl.ds(0, NB)].reshape(N, H)
    me = lax.axis_index("sub")
    for d, o in enumerate((o0, o1, o2, o3, o4, o5)):
        q = lax.rem(me + d, SUB) if d < SUB else d
        o[...] = total[NB + q].astype(BF16)


def land_kernel(rows_ref, count_ref, r0, r1, r2, r3, r4, r5, own_ref, out_ref):
    me = lax.axis_index("sub")
    lane = lax.broadcasted_iota(jnp.int32, (1, BLK), 1)
    ids = []
    for d in range(PEERS):
        q = lax.rem(me + SUB - d, SUB) if d < SUB else d
        ids.append(jnp.where(lane < count_ref[0, q], rows_ref[q], -1))
    ids = jnp.concatenate(ids, axis=1)
    back = jnp.concatenate([r[...] for r in (r0, r1, r2, r3, r4, r5)], axis=0)
    for c in range(N // CH):
        rows = pl.ds(c * CH, CH)
        hot = lax.broadcasted_iota(jnp.int32, (CH, PEERS * BLK), 0) + c * CH == ids
        hot = jnp.where(hot, 1.0, 0.0).astype(BF16)
        out_ref[rows, :] = own_ref[rows, :] + dot(hot, back)


def fold_kernel(parts, out_ref):
    out_ref[...] = jnp.sum(parts[...].astype(F32), axis=0).astype(BF16)


def pair_kernel(mine, other, out_ref):
    both = (mine[...].astype(F32) + other[...].astype(F32)).astype(BF16)
    for i in range(out_ref.shape[0]):
        out_ref[i] = both


def spread_kernel(parts, out_ref):
    whole = jnp.sum(parts[...].astype(F32), axis=0).astype(BF16)
    for i in range(out_ref.shape[0]):
        out_ref[i] = whole


def clip_kernel(parts, in_ref, bias_ref, out_ref):
    squares = jnp.zeros((8, H), F32)
    for k in range(CHUNKS):
        piece = parts[k].astype(F32)
        squares = squares + jnp.sum(jnp.square(piece[:48]).reshape(6, 8, H), axis=0)
    bias = parts[0].astype(F32)[48:49]
    norm = jnp.sum(squares, keepdims=True) + jnp.sum(jnp.square(bias), keepdims=True)
    factor = jnp.minimum(1.0, clip_norm * lax.rsqrt(norm + 1e-06))
    for k in range(CHUNKS):
        piece = parts[k].astype(F32) * factor
        in_ref[pl.ds(32 * k, 32), :] = piece[:32]
        out_ref[pl.ds(16 * k, 16), :] = piece[32:48]
    bias_ref[...] = bias * factor


def shift(value, axis, by, size):
    return lax.ppermute(value, axis, [(i, (i + by) % size) for i in range(size)])


def exchange(slots):
    got = [slots[0]]
    got += [shift(slots[d], "sub", d, SUB) for d in range(1, SUB)]
    dom = 1
    for axis in DOM:
        dom *= lax.axis_size(axis)
    return got, dom


def local(feat, cot, vals, src, dst, halo_rows, halo_count, w_in, b_in, w_out):
    block = sds((BLK, H), BF16)
    by_slot = jnp.transpose(halo_rows, (1, 0, 2))
    slots = pl.pallas_call(
        pick_kernel,
        out_shape=[block] * PEERS,
        in_specs=[HB] * 3,
        out_specs=[VM] * PEERS,
        scratch_shapes=[
            pltpu.VMEM((PEERS, 1, BLK), jnp.int32),
            pltpu.SMEM((1, PEERS), jnp.int32),
            pltpu.VMEM((N, H), BF16),
            pltpu.VMEM((PEERS * BLK, N), BF16),
            pltpu.SemaphoreType.DMA((3,)),
        ],
        compiler_params=params(24),
        name="pick",
    )(*[pltpu.with_memory_space_constraint(v, pltpu.HBM) for v in (by_slot, halo_count, feat)])
    got, dom = exchange(slots)
    got += [shift(slots[4], DOM, 1, dom), shift(slots[5], DOM, -1, dom)]
    near = pl.pallas_call(
        near_kernel,
        out_shape=sds((NB + 1, BLK, H), F32),
        in_specs=[HB] * 4,
        out_specs=VM,
        scratch_shapes=[
            pltpu.SMEM((T,), jnp.int32),
            pltpu.SMEM((T,), jnp.int32),
            pltpu.SMEM((T + NEAR_STEP,), jnp.int32),
            pltpu.VMEM((N, H), BF16),
            pltpu.VMEM((T, BLK, BLK), BF16),
            pltpu.SemaphoreType.DMA((4,)),
        ],
        compiler_params=params(24),
        cost_estimate=pl.CostEstimate(flops=800_000_000, bytes_accessed=6_000_000, transcendentals=0),
        name="near",
    )(*[pltpu.with_memory_space_constraint(v, pltpu.HBM) for v in (src, dst, feat, vals)])
    new_rows, gpre, pay = pl.pallas_call(
        node_kernel,
        out_shape=[sds((N, H), BF16), sds((N, H), BF16), sds((CHUNKS, CROWS, H), BF16)],
        in_specs=[SM, SM] + [VM] * 13,
        out_specs=[VM] * 3,
        scratch_shapes=[
            pltpu.SMEM((T + NEAR_STEP,), jnp.int32),
            pltpu.VMEM((PEERS, BLK, H), BF16),
            pltpu.VMEM((NB + 1, BLK, H), F32),
            pltpu.VMEM((2 * H, H), F32),
            pltpu.VMEM((H, H), F32),
        ],
        compiler_params=params(32),
        name="node",
    )(src, dst, *got, feat, cot, vals, near, w_in, b_in.reshape(1, H), w_out)
    parts = lax.all_to_all(pay, PLANE, split_axis=0, concat_axis=0, tiled=True)
    back = pl.pallas_call(
        back_kernel,
        out_shape=[sds((N, H), F32)] + [block] * PEERS,
        in_specs=[SM, SM] + [VM] * 4,
        out_specs=[VM] * 7,
        scratch_shapes=[pltpu.VMEM((N, H), BF16), pltpu.VMEM((BUF, BLK, H), F32)],
        compiler_params=params(32),
        cost_estimate=pl.CostEstimate(flops=4_000_000_000, bytes_accessed=9_000_000, transcendentals=0),
        name="back",
    )(src, dst, gpre, cot, vals, w_in)
    own, slots = back[0], back[1:]
    parts, own = lax.optimization_barrier((parts, own))
    piece = sds((CROWS, H), BF16)
    folded = pl.pallas_call(
        fold_kernel, out_shape=piece, in_specs=[VM], out_specs=VM, compiler_params=params(4), name="fold"
    )(parts)
    other = shift(folded, "core", 1, 2)
    depth = lax.axis_size("z")
    paired = pl.pallas_call(
        pair_kernel,
        out_shape=sds((depth, CROWS, H), BF16),
        in_specs=[VM] * 2,
        out_specs=VM,
        compiler_params=params(4),
        name="pair",
    )(folded, other)
    paired, *slots = lax.optimization_barrier((paired, *slots))
    column = lax.all_to_all(paired, "z", split_axis=0, concat_axis=0, tiled=True)
    got, dom = exchange(slots)
    got += [shift(slots[4], DOM, -1, dom), shift(slots[5], DOM, 1, dom)]
    column, *got = lax.optimization_barrier((column, *got))
    spread = pl.pallas_call(
        spread_kernel,
        out_shape=sds((CHUNKS, CROWS, H), BF16),
        in_specs=[VM],
        out_specs=VM,
        compiler_params=params(4),
        name="spread",
    )(column)
    whole = lax.all_to_all(spread, PLANE, split_axis=0, concat_axis=0, tiled=True)
    grad_features = pl.pallas_call(
        land_kernel,
        out_shape=sds((N, H), F32),
        in_specs=[VM, SM] + [VM] * 7,
        out_specs=VM,
        compiler_params=params(24),
        cost_estimate=pl.CostEstimate(flops=3_000_000_000, bytes_accessed=5_000_000, transcendentals=0),
        name="land",
    )(by_slot, halo_count, *got, own)
    whole, grad_features = lax.optimization_barrier((whole, grad_features))
    g_in, g_bias, g_out = pl.pallas_call(
        clip_kernel,
        out_shape=[sds((2 * H, H), F32), sds((1, H), F32), sds((H, H), F32)],
        in_specs=[VM],
        out_specs=[VM] * 3,
        compiler_params=params(8),
        name="clip",
    )(whole)
    return new_rows, grad_features, g_in, g_bias.reshape(H), g_out


def solution(mesh):
    grid = Mesh(mesh.devices.reshape(4, 8, 2, 4), ALL)
    split2, split1 = P(ALL, None), P(ALL)
    split3 = P(ALL, None, None)
    return jax.shard_map(
        local,
        mesh=grid,
        in_specs=(split2, split2, split3, split1, split1, split3, split2, P(), P(), P()),
        out_specs=(split2, split2, P(), P(), P()),
        check_vma=False,
    )
```

```python
import jax
import jax.numpy as jnp
from jax import lax
from jax.experimental import pallas as pl
from jax.experimental.pallas import tpu as pltpu
from jax.sharding import Mesh, PartitionSpec as P

H = 256
BLK = 128
NB = 16
N = NB * BLK
T = 64
PEERS = 6
SUB = 4
BUF = NB + PEERS
CHUNKS = 16
PROWS = 56
HALF = H // 2
CH = 1024
NEAR_STEP = 16
FAR_STEP = 8
BACK_STEP = 32
clip_norm = 256.0
ln_eps = 1e-05
F32 = jnp.float32
BF16 = jnp.bfloat16
ALL = ("x", "z", "core", "sub")
DOM = ("x", "z", "core")
PLANE = ("x", "sub")
MIB = 1024 * 1024
VM = pl.BlockSpec(memory_space=pltpu.VMEM)
HB = pl.BlockSpec(memory_space=pltpu.HBM)
SM = pl.BlockSpec(memory_space=pltpu.SMEM)


def params(mib):
    return pltpu.CompilerParams(vmem_limit_bytes=mib * MIB)


def sds(shape, dtype):
    return jax.ShapeDtypeStruct(shape, dtype)


def dot(a, b):
    return jnp.dot(a, b, preferred_element_type=F32)


def dot_t0(a, b):
    return lax.dot_general(a, b, (((0,), (0,)), ((), ())), preferred_element_type=F32)


def dot_t1(a, b):
    return lax.dot_general(a, b, (((1,), (1,)), ((), ())), preferred_element_type=F32)


def pick_kernel(rows_hbm, count_hbm, feat_hbm, o0, o1, o2, o3, o4, o5, rows, count, feat, hot, sems):
    load_rows = pltpu.make_async_copy(rows_hbm, rows, sems.at[0])
    load_count = pltpu.make_async_copy(count_hbm, count, sems.at[1])
    load_feat = pltpu.make_async_copy(feat_hbm, feat, sems.at[2])
    load_rows.start()
    load_count.start()
    load_feat.start()
    me = lax.axis_index("sub")
    load_rows.wait()
    load_count.wait()
    lane = lax.broadcasted_iota(jnp.int32, (1, BLK), 1)
    node = lax.broadcasted_iota(jnp.int32, (BLK, N), 1)
    for d in range(PEERS):
        q = lax.rem(me + d, SUB) if d < SUB else d
        ids = jnp.where(lane < count[0, q], rows[q], -1)
        column = jnp.transpose(jnp.broadcast_to(ids, (8, BLK)))[:, :1]
        hot[pl.ds(d * BLK, BLK), :] = jnp.where(node == column, 1.0, 0.0).astype(BF16)
    load_feat.wait()
    picked = dot(hot[...], feat[...]).astype(BF16)
    for d, o in enumerate((o0, o1, o2, o3, o4, o5)):
        o[...] = picked[d * BLK : (d + 1) * BLK]


def list_tiles(src_ref, dst_ref, listed, least, most, spare):
    def step(t, n):
        s = src_ref[t]
        listed[n] = (dst_ref[t] * 32 + s) * 64 + t
        return n + jnp.where((s >= least) & (s < most), 1, 0)

    n = lax.fori_loop(0, T, step, jnp.int32(0), unroll=True)
    for p in range(spare):
        listed[n + p] = (NB * 32 + least) * 64
    return n


def near_kernel(src_hbm, dst_hbm, feat_hbm, vals_hbm, total, src, dst, listed, feat, vals, sems):
    load_src = pltpu.make_async_copy(src_hbm, src, sems.at[0])
    load_dst = pltpu.make_async_copy(dst_hbm, dst, sems.at[1])
    load_feat = pltpu.make_async_copy(feat_hbm, feat, sems.at[2])
    load_vals = pltpu.make_async_copy(vals_hbm, vals, sems.at[3])
    load_src.start()
    load_dst.start()
    load_feat.start()
    load_vals.start()
    total[...] = jnp.zeros_like(total)
    load_src.wait()
    load_dst.wait()
    n = list_tiles(src, dst, listed, 0, NB, NEAR_STEP)
    load_feat.wait()
    load_vals.wait()

    def step(i, _):
        for u in range(NEAR_STEP):
            packed = listed[i * NEAR_STEP + u]
            t, s, d = packed % 64, (packed // 64) % 32, packed // 2048
            rows = feat[pl.ds(pl.multiple_of(s * BLK, BLK), BLK), :]
            total[d] += dot(vals[t], rows)
        return 0

    lax.fori_loop(0, pl.cdiv(n, NEAR_STEP), step, 0)


def node_kernel(
    src_ref, dst_ref, h0, h1, h2, h3, h4, h5, feat_ref, cot_ref, vals_ref, near_ref,
    win_ref, bin_ref, wout_ref, new_ref, gpre_ref, keep_ref, give_ref, listed, halo, total, sum_in, sum_out,
):
    n = list_tiles(src_ref, dst_ref, listed, NB, BUF, FAR_STEP)
    me = lax.axis_index("sub")
    for d, h in enumerate((h0, h1, h2, h3, h4, h5)):
        q = lax.rem(me + SUB - d, SUB) if d < SUB else d
        halo[q] = h[...]
    total[...] = near_ref[...]

    def step(i, _):
        for u in range(FAR_STEP):
            packed = listed[i * FAR_STEP + u]
            t, s, d = packed % 64, (packed // 64) % 32, packed // 2048
            total[d] += dot(vals_ref[t], halo[s - NB])
        return 0

    lax.fori_loop(0, pl.cdiv(n, FAR_STEP), step, 0)
    w_in, b_in, w_out = win_ref[...], bin_ref[...], wout_ref[...]
    sum_bias = jnp.zeros((1, H), F32)
    for c in range(N // CH):
        rows = pl.ds(c * CH, CH)
        per = CH // BLK
        agg = total[pl.ds(c * per, per)].reshape(CH, H).astype(BF16)
        feat = feat_ref[rows, :]
        joined = jnp.concatenate([feat, agg], axis=1)
        pre = dot(joined, w_in) + b_in
        sig = 1.0 / (1.0 + jnp.exp(-pre))
        act = (pre * sig).astype(BF16)
        slope = sig * (1.0 + pre * (1.0 - sig))
        lifted = dot(act, w_out)
        centred = lifted - jnp.mean(lifted, axis=1, keepdims=True)
        inv_std = lax.rsqrt(jnp.mean(centred * centred, axis=1, keepdims=True) + ln_eps)
        normed = centred * inv_std
        new_ref[rows, :] = (feat.astype(F32) + normed).astype(BF16)
        up = cot_ref[rows, :].astype(F32)
        grad_lifted = inv_std * (
            up
            - jnp.mean(up, axis=1, keepdims=True)
            - normed * jnp.mean(up * normed, axis=1, keepdims=True)
        )
        grad_lifted = grad_lifted.astype(BF16)
        gpre = (dot_t1(grad_lifted, w_out) * slope).astype(BF16)
        gpre_ref[rows, :] = gpre
        g_out = dot_t0(act, grad_lifted)
        g_in = dot_t0(joined, gpre)
        sum_bias = sum_bias + jnp.sum(gpre.astype(F32), axis=0, keepdims=True)
        if c == 0:
            sum_in[...] = g_in
            sum_out[...] = g_out
        else:
            sum_in[...] += g_in
            sum_out[...] += g_out
    bias = jnp.concatenate([sum_bias[:, :HALF], sum_bias[:, HALF:], jnp.zeros((6, HALF), F32)], axis=0)
    mine = lax.axis_index("core")
    for half, out in ((mine, keep_ref), (1 - mine, give_ref)):
        for k in range(CHUNKS):
            top = sum_in[pl.ds(pl.multiple_of(32 * k + 16 * half, 8), 16), :]
            low = sum_out[pl.ds(pl.multiple_of(16 * k + 8 * half, 8), 8), :]
            last = bias if k == 0 else jnp.zeros((8, HALF), F32)
            piece = jnp.concatenate(
                [top[:, :HALF], low[:, :HALF], top[:, HALF:], low[:, HALF:], last], axis=0
            )
            out[k] = piece.astype(out.dtype)


def back_kernel(
    src_ref, dst_ref, gpre_ref, cot_ref, vals_ref, win_ref, own_ref, o0, o1, o2, o3, o4, o5, grad_agg, total
):
    w_in = win_ref[...]
    for c in range(N // CH):
        rows = pl.ds(c * CH, CH)
        per = CH // BLK
        joined = dot_t1(gpre_ref[rows, :], w_in)
        grad_agg[rows, :] = joined[:, H:].astype(BF16)
        direct = cot_ref[rows, :].astype(F32) + joined[:, :H]
        total[pl.ds(c * per, per)] = direct.reshape(per, BLK, H)
    total[pl.ds(NB, PEERS)] = jnp.zeros((PEERS, BLK, H), F32)

    def step(i, _):
        for u in range(BACK_STEP):
            t = i * BACK_STEP + u
            s, d = src_ref[t], dst_ref[t]
            down = grad_agg[pl.ds(pl.multiple_of(d * BLK, BLK), BLK), :]
            total[s] += dot_t0(vals_ref[t], down)
        return 0

    lax.fori_loop(0, T // BACK_STEP, step, 0)
    own_ref[...] = total[pl.ds(0, NB)].reshape(N, H)
    me = lax.axis_index("sub")
    for d, o in enumerate((o0, o1, o2, o3, o4, o5)):
        q = lax.rem(me + d, SUB) if d < SUB else d
        o[...] = total[NB + q].astype(BF16)


def land_kernel(rows_ref, count_ref, r0, r1, r2, r3, r4, r5, own_ref, out_ref):
    me = lax.axis_index("sub")
    lane = lax.broadcasted_iota(jnp.int32, (1, BLK), 1)
    ids = []
    for d in range(PEERS):
        q = lax.rem(me + SUB - d, SUB) if d < SUB else d
        ids.append(jnp.where(lane < count_ref[0, q], rows_ref[q], -1))
    ids = jnp.concatenate(ids, axis=1)
    back = jnp.concatenate([r[...] for r in (r0, r1, r2, r3, r4, r5)], axis=0)
    for c in range(N // CH):
        rows = pl.ds(c * CH, CH)
        hot = lax.broadcasted_iota(jnp.int32, (CH, PEERS * BLK), 0) + c * CH == ids
        hot = jnp.where(hot, 1.0, 0.0).astype(BF16)
        out_ref[rows, :] = own_ref[rows, :] + dot(hot, back)


def join_kernel(keep, other, out_ref):
    out_ref[...] = (keep[...] + other[...].astype(F32)).astype(BF16)


def spread_kernel(parts, out_ref):
    whole = jnp.sum(parts[...].astype(F32), axis=0).astype(BF16)
    for i in range(out_ref.shape[0]):
        out_ref[i] = whole


def clip_kernel(keep, other, in_ref, bias_ref, out_ref):
    norms = []
    for part in (keep, other):
        squares = jnp.zeros((8, HALF), F32)
        for k in range(CHUNKS):
            piece = part[k].astype(F32)[:48]
            squares = squares + jnp.sum(jnp.square(piece).reshape(6, 8, HALF), axis=0)
        norms.append(jnp.sum(squares, keepdims=True))
    last = keep[0].astype(F32)[48:56]
    mine = lax.axis_index("core")
    last = jnp.where(mine == 0, last, other[0].astype(F32)[48:56])
    norm = norms[0] + norms[1] + jnp.sum(jnp.square(last), keepdims=True)
    factor = jnp.minimum(1.0, clip_norm * lax.rsqrt(norm + 1e-06))
    for half, part in ((mine, keep), (1 - mine, other)):
        for k in range(CHUNKS):
            piece = part[k].astype(F32) * factor
            top = jnp.concatenate([piece[0:16], piece[24:40]], axis=1)
            low = jnp.concatenate([piece[16:24], piece[40:48]], axis=1)
            in_ref[pl.ds(pl.multiple_of(32 * k + 16 * half, 8), 16), :] = top
            out_ref[pl.ds(pl.multiple_of(16 * k + 8 * half, 8), 8), :] = low
    bias_ref[...] = jnp.concatenate([last[0:1], last[1:2]], axis=1) * factor


def shift(value, axis, by, size):
    return lax.ppermute(value, axis, [(i, (i + by) % size) for i in range(size)])


def exchange(slots):
    got = [slots[0]]
    got += [shift(slots[d], "sub", d, SUB) for d in range(1, SUB)]
    dom = 1
    for axis in DOM:
        dom *= lax.axis_size(axis)
    return got, dom


def local(feat, cot, vals, src, dst, halo_rows, halo_count, w_in, b_in, w_out):
    block = sds((BLK, H), BF16)
    halves = (CHUNKS, PROWS, HALF)
    by_slot = jnp.transpose(halo_rows, (1, 0, 2))
    slots = pl.pallas_call(
        pick_kernel,
        out_shape=[block] * PEERS,
        in_specs=[HB] * 3,
        out_specs=[VM] * PEERS,
        scratch_shapes=[
            pltpu.VMEM((PEERS, 1, BLK), jnp.int32),
            pltpu.SMEM((1, PEERS), jnp.int32),
            pltpu.VMEM((N, H), BF16),
            pltpu.VMEM((PEERS * BLK, N), BF16),
            pltpu.SemaphoreType.DMA((3,)),
        ],
        compiler_params=params(24),
        name="pick",
    )(*[pltpu.with_memory_space_constraint(v, pltpu.HBM) for v in (by_slot, halo_count, feat)])
    got, dom = exchange(slots)
    got += [shift(slots[4], DOM, 1, dom), shift(slots[5], DOM, -1, dom)]
    near = pl.pallas_call(
        near_kernel,
        out_shape=sds((NB + 1, BLK, H), F32),
        in_specs=[HB] * 4,
        out_specs=VM,
        scratch_shapes=[
            pltpu.SMEM((T,), jnp.int32),
            pltpu.SMEM((T,), jnp.int32),
            pltpu.SMEM((T + NEAR_STEP,), jnp.int32),
            pltpu.VMEM((N, H), BF16),
            pltpu.VMEM((T, BLK, BLK), BF16),
            pltpu.SemaphoreType.DMA((4,)),
        ],
        compiler_params=params(24),
        cost_estimate=pl.CostEstimate(flops=800_000_000, bytes_accessed=6_000_000, transcendentals=0),
        name="near",
    )(*[pltpu.with_memory_space_constraint(v, pltpu.HBM) for v in (src, dst, feat, vals)])
    new_rows, gpre, keep, give = pl.pallas_call(
        node_kernel,
        out_shape=[sds((N, H), BF16), sds((N, H), BF16), sds(halves, F32), sds(halves, BF16)],
        in_specs=[SM, SM] + [VM] * 13,
        out_specs=[VM] * 4,
        scratch_shapes=[
            pltpu.SMEM((T + NEAR_STEP,), jnp.int32),
            pltpu.VMEM((PEERS, BLK, H), BF16),
            pltpu.VMEM((NB + 1, BLK, H), F32),
            pltpu.VMEM((2 * H, H), F32),
            pltpu.VMEM((H, H), F32),
        ],
        compiler_params=params(32),
        name="node",
    )(src, dst, *got, feat, cot, vals, near, w_in, b_in.reshape(1, H), w_out)
    given = shift(give, "core", 1, 2)
    joined = pl.pallas_call(
        join_kernel, out_shape=sds(halves, BF16), in_specs=[VM] * 2, out_specs=VM, compiler_params=params(4), name="join"
    )(keep, given)
    parts = lax.all_to_all(joined, PLANE, split_axis=0, concat_axis=0, tiled=True)
    back = pl.pallas_call(
        back_kernel,
        out_shape=[sds((N, H), F32)] + [block] * PEERS,
        in_specs=[SM, SM] + [VM] * 4,
        out_specs=[VM] * 7,
        scratch_shapes=[pltpu.VMEM((N, H), BF16), pltpu.VMEM((BUF, BLK, H), F32)],
        compiler_params=params(32),
        cost_estimate=pl.CostEstimate(flops=4_000_000_000, bytes_accessed=9_000_000, transcendentals=0),
        name="back",
    )(src, dst, gpre, cot, vals, w_in)
    own, slots = back[0], back[1:]
    parts, own = lax.optimization_barrier((parts, own))
    depth = lax.axis_size("z")
    paired = pl.pallas_call(
        spread_kernel,
        out_shape=sds((depth, PROWS, HALF), BF16),
        in_specs=[VM],
        out_specs=VM,
        compiler_params=params(4),
        name="fold",
    )(parts)
    paired, *slots = lax.optimization_barrier((paired, *slots))
    column = lax.all_to_all(paired, "z", split_axis=0, concat_axis=0, tiled=True)
    got, dom = exchange(slots)
    got += [shift(slots[4], DOM, -1, dom), shift(slots[5], DOM, 1, dom)]
    column, *got = lax.optimization_barrier((column, *got))
    spread = pl.pallas_call(
        spread_kernel,
        out_shape=sds(halves, BF16),
        in_specs=[VM],
        out_specs=VM,
        compiler_params=params(4),
        name="spread",
    )(column)
    whole = lax.all_to_all(spread, PLANE, split_axis=0, concat_axis=0, tiled=True)
    grad_features = pl.pallas_call(
        land_kernel,
        out_shape=sds((N, H), F32),
        in_specs=[VM, SM] + [VM] * 7,
        out_specs=VM,
        compiler_params=params(24),
        cost_estimate=pl.CostEstimate(flops=3_000_000_000, bytes_accessed=5_000_000, transcendentals=0),
        name="land",
    )(by_slot, halo_count, *got, own)
    whole, grad_features = lax.optimization_barrier((whole, grad_features))
    other = shift(whole, "core", 1, 2)
    g_in, g_bias, g_out = pl.pallas_call(
        clip_kernel,
        out_shape=[sds((2 * H, H), F32), sds((1, H), F32), sds((H, H), F32)],
        in_specs=[VM] * 2,
        out_specs=[VM] * 3,
        compiler_params=params(8),
        name="clip",
    )(whole, other)
    return new_rows, grad_features, g_in, g_bias.reshape(H), g_out


def solution(mesh):
    grid = Mesh(mesh.devices.reshape(4, 8, 2, 4), ALL)
    split2, split1 = P(ALL, None), P(ALL)
    split3 = P(ALL, None, None)
    return jax.shard_map(
        local,
        mesh=grid,
        in_specs=(split2, split2, split3, split1, split1, split3, split2, P(), P(), P()),
        out_specs=(split2, split2, P(), P(), P()),
        check_vma=False,
    )
```

```python
import jax
import jax.numpy as jnp
from jax import lax
from jax.experimental import pallas as pl
from jax.experimental.pallas import tpu as pltpu
from jax.sharding import Mesh, PartitionSpec as P

H = 256
BLK = 128
NB = 16
N = NB * BLK
T = 64
PEERS = 6
SUB = 4
BUF = NB + PEERS
CHUNKS = 16
PROWS = 56
HALF = H // 2
CH = 1024
NEAR_STEP = 16
FAR_STEP = 8
BACK = 512
BACK_STEP = 64
LAND = 512
clip_norm = 256.0
ln_eps = 1e-05
F32 = jnp.float32
BF16 = jnp.bfloat16
ALL = ("x", "z", "core", "sub")
DOM = ("x", "z", "core")
PLANE = ("x", "sub")
MIB = 1024 * 1024
VM = pl.BlockSpec(memory_space=pltpu.VMEM)
HB = pl.BlockSpec(memory_space=pltpu.HBM)
SM = pl.BlockSpec(memory_space=pltpu.SMEM)


def params(mib):
    return pltpu.CompilerParams(vmem_limit_bytes=mib * MIB)


def sds(shape, dtype):
    return jax.ShapeDtypeStruct(shape, dtype)


def dot(a, b):
    return jnp.dot(a, b, preferred_element_type=F32)


def dot_t0(a, b):
    return lax.dot_general(a, b, (((0,), (0,)), ((), ())), preferred_element_type=F32)


def dot_t1(a, b):
    return lax.dot_general(a, b, (((1,), (1,)), ((), ())), preferred_element_type=F32)


def pick_kernel(rows_hbm, count_hbm, feat_hbm, o0, o1, o2, o3, o4, o5, rows, count, feat, hot, sems):
    load_rows = pltpu.make_async_copy(rows_hbm, rows, sems.at[0])
    load_count = pltpu.make_async_copy(count_hbm, count, sems.at[1])
    load_feat = pltpu.make_async_copy(feat_hbm, feat, sems.at[2])
    load_rows.start()
    load_count.start()
    load_feat.start()
    me = lax.axis_index("sub")
    load_rows.wait()
    load_count.wait()
    lane = lax.broadcasted_iota(jnp.int32, (1, BLK), 1)
    node = lax.broadcasted_iota(jnp.int32, (BLK, N), 1)
    for d in range(PEERS):
        q = lax.rem(me + d, SUB) if d < SUB else d
        ids = jnp.where(lane < count[0, q], rows[q], -1)
        column = jnp.transpose(jnp.broadcast_to(ids, (8, BLK)))[:, :1]
        hot[pl.ds(d * BLK, BLK), :] = jnp.where(node == column, 1.0, 0.0).astype(BF16)
    load_feat.wait()
    picked = dot(hot[...], feat[...]).astype(BF16)
    for d, o in enumerate((o0, o1, o2, o3, o4, o5)):
        o[...] = picked[d * BLK : (d + 1) * BLK]


def list_tiles(src_ref, dst_ref, listed, least, most, spare):
    def step(t, n):
        s = src_ref[t]
        listed[n] = (dst_ref[t] * 32 + s) * 64 + t
        return n + jnp.where((s >= least) & (s < most), 1, 0)

    n = lax.fori_loop(0, T, step, jnp.int32(0), unroll=True)
    for p in range(spare):
        listed[n + p] = (NB * 32 + least) * 64
    return n


def near_kernel(src_hbm, dst_hbm, feat_hbm, vals_hbm, total, src, dst, listed, feat, vals, sems):
    load_src = pltpu.make_async_copy(src_hbm, src, sems.at[0])
    load_dst = pltpu.make_async_copy(dst_hbm, dst, sems.at[1])
    load_feat = pltpu.make_async_copy(feat_hbm, feat, sems.at[2])
    load_vals = pltpu.make_async_copy(vals_hbm, vals, sems.at[3])
    load_src.start()
    load_dst.start()
    load_feat.start()
    load_vals.start()
    total[...] = jnp.zeros_like(total)
    load_src.wait()
    load_dst.wait()
    n = list_tiles(src, dst, listed, 0, NB, NEAR_STEP)
    load_feat.wait()
    load_vals.wait()

    def step(i, _):
        for u in range(NEAR_STEP):
            packed = listed[i * NEAR_STEP + u]
            t, s, d = packed % 64, (packed // 64) % 32, packed // 2048
            rows = feat[pl.ds(pl.multiple_of(s * BLK, BLK), BLK), :]
            total[d] += dot(vals[t], rows)
        return 0

    lax.fori_loop(0, pl.cdiv(n, NEAR_STEP), step, 0)


def node_kernel(
    src_ref, dst_ref, h0, h1, h2, h3, h4, h5, feat_ref, cot_ref, vals_ref, near_ref,
    win_ref, bin_ref, wout_ref, new_hbm, gpre_hbm, keep_ref, give_ref, listed, halo, total, sum_in, sum_out,
    new_rows, grad_pre, sems,
):
    n = list_tiles(src_ref, dst_ref, listed, NB, BUF, FAR_STEP)
    me = lax.axis_index("sub")
    for d, h in enumerate((h0, h1, h2, h3, h4, h5)):
        q = lax.rem(me + SUB - d, SUB) if d < SUB else d
        halo[q] = h[...]
    total[...] = near_ref[...]

    def step(i, _):
        for u in range(FAR_STEP):
            packed = listed[i * FAR_STEP + u]
            t, s, d = packed % 64, (packed // 64) % 32, packed // 2048
            total[d] += dot(vals_ref[t], halo[s - NB])
        return 0

    lax.fori_loop(0, pl.cdiv(n, FAR_STEP), step, 0)
    w_in, b_in, w_out = win_ref[...], bin_ref[...], wout_ref[...]
    sum_bias = jnp.zeros((1, H), F32)
    stores = []
    for c in range(N // CH):
        rows = pl.ds(c * CH, CH)
        per = CH // BLK
        agg = total[pl.ds(c * per, per)].reshape(CH, H).astype(BF16)
        feat = feat_ref[rows, :]
        joined = jnp.concatenate([feat, agg], axis=1)
        pre = dot(joined, w_in) + b_in
        sig = 1.0 / (1.0 + jnp.exp(-pre))
        act = (pre * sig).astype(BF16)
        slope = sig * (1.0 + pre * (1.0 - sig))
        lifted = dot(act, w_out)
        centred = lifted - jnp.mean(lifted, axis=1, keepdims=True)
        inv_std = lax.rsqrt(jnp.mean(centred * centred, axis=1, keepdims=True) + ln_eps)
        normed = centred * inv_std
        new_rows[rows, :] = (feat.astype(F32) + normed).astype(BF16)
        store = pltpu.make_async_copy(new_rows.at[rows, :], new_hbm.at[rows, :], sems.at[0, c])
        store.start()
        stores.append(store)
        up = cot_ref[rows, :].astype(F32)
        grad_lifted = inv_std * (
            up
            - jnp.mean(up, axis=1, keepdims=True)
            - normed * jnp.mean(up * normed, axis=1, keepdims=True)
        )
        grad_lifted = grad_lifted.astype(BF16)
        gpre = (dot_t1(grad_lifted, w_out) * slope).astype(BF16)
        grad_pre[rows, :] = gpre
        store = pltpu.make_async_copy(grad_pre.at[rows, :], gpre_hbm.at[rows, :], sems.at[1, c])
        store.start()
        stores.append(store)
        g_out = dot_t0(act, grad_lifted)
        g_in = dot_t0(joined, gpre)
        sum_bias = sum_bias + jnp.sum(gpre.astype(F32), axis=0, keepdims=True)
        if c == 0:
            sum_in[...] = g_in
            sum_out[...] = g_out
        else:
            sum_in[...] += g_in
            sum_out[...] += g_out
    bias = jnp.concatenate([sum_bias[:, :HALF], sum_bias[:, HALF:], jnp.zeros((6, HALF), F32)], axis=0)
    mine = lax.axis_index("core")
    for half, out in ((mine, keep_ref), (1 - mine, give_ref)):
        for k in range(CHUNKS):
            top = sum_in[pl.ds(pl.multiple_of(32 * k + 16 * half, 8), 16), :]
            low = sum_out[pl.ds(pl.multiple_of(16 * k + 8 * half, 8), 8), :]
            last = bias if k == 0 else jnp.zeros((8, HALF), F32)
            piece = jnp.concatenate(
                [top[:, :HALF], low[:, :HALF], top[:, HALF:], low[:, HALF:], last], axis=0
            )
            out[k] = piece.astype(out.dtype)
    for store in stores:
        store.wait()


def back_kernel(
    src_ref, dst_ref, vals_ref, gpre_hbm, win_hbm, cot_hbm, own_hbm, o0, o1, o2, o3, o4, o5,
    gpre, win, cot, grad_agg, total, sems,
):
    loads = [
        pltpu.make_async_copy(win_hbm, win, sems.at[0]),
        pltpu.make_async_copy(gpre_hbm, gpre, sems.at[1]),
        pltpu.make_async_copy(cot_hbm, cot, sems.at[2]),
    ]
    for load in loads:
        load.start()
    total[pl.ds(NB, PEERS)] = jnp.zeros((PEERS, BLK, H), F32)
    for load in loads:
        load.wait()
    w_in = win[...]
    per = BACK // BLK
    for c in range(N // BACK):
        rows = pl.ds(c * BACK, BACK)
        joined = dot_t1(gpre[rows, :], w_in)
        grad_agg[rows, :] = joined[:, H:].astype(BF16)
        direct = cot[rows, :].astype(F32) + joined[:, :H]
        total[pl.ds(c * per, per)] = direct.reshape(per, BLK, H)

    def step(i, _):
        for u in range(BACK_STEP):
            t = i * BACK_STEP + u
            s, d = src_ref[t], dst_ref[t]
            down = grad_agg[pl.ds(pl.multiple_of(d * BLK, BLK), BLK), :]
            total[s] += dot_t0(vals_ref[t], down)
        return 0

    lax.fori_loop(0, T // BACK_STEP, step, 0)
    store = pltpu.make_async_copy(total.at[pl.ds(0, NB)], own_hbm, sems.at[3])
    store.start()
    me = lax.axis_index("sub")
    for d, o in enumerate((o0, o1, o2, o3, o4, o5)):
        q = lax.rem(me + d, SUB) if d < SUB else d
        o[...] = total[NB + q].astype(BF16)
    store.wait()


def land_kernel(
    rows_hbm, count_hbm, r0, r1, r2, r3, r4, r5, own_hbm, out_hbm, rows_ref, count, own, sems
):
    loads = [
        pltpu.make_async_copy(rows_hbm, rows_ref, sems.at[0]),
        pltpu.make_async_copy(count_hbm, count, sems.at[1]),
        pltpu.make_async_copy(own_hbm, own, sems.at[2]),
    ]
    for load in loads:
        load.start()
    for load in loads[:2]:
        load.wait()
    me = lax.axis_index("sub")
    lane = lax.broadcasted_iota(jnp.int32, (1, BLK), 1)
    ids = []
    for d in range(PEERS):
        q = lax.rem(me + SUB - d, SUB) if d < SUB else d
        ids.append(jnp.where(lane < count[0, q], rows_ref[q], -1))
    ids = jnp.concatenate(ids, axis=1)
    back = jnp.concatenate([r[...] for r in (r0, r1, r2, r3, r4, r5)], axis=0)
    stores = []
    for c in range(N // LAND):
        node = lax.broadcasted_iota(jnp.int32, (LAND, PEERS * BLK), 0) + c * LAND
        hot = jnp.where(node == ids, 1.0, 0.0).astype(BF16)
        landed = dot(hot, back)
        if c == 0:
            loads[2].wait()
        per = LAND // BLK
        blocks = pl.ds(c * per, per)
        own[blocks] += landed.reshape(per, BLK, H)
        store = pltpu.make_async_copy(own.at[blocks], out_hbm.at[blocks], sems.at[3 + c])
        store.start()
        stores.append(store)
    for store in stores:
        store.wait()


def join_kernel(keep, other, out_ref):
    out_ref[...] = (keep[...] + other[...].astype(F32)).astype(BF16)


def spread_kernel(parts, out_ref):
    whole = jnp.sum(parts[...].astype(F32), axis=0).astype(BF16)
    for i in range(out_ref.shape[0]):
        out_ref[i] = whole


def clip_kernel(keep, other, in_ref, bias_ref, out_ref):
    norms = []
    for part in (keep, other):
        squares = jnp.zeros((8, HALF), F32)
        for k in range(CHUNKS):
            piece = part[k].astype(F32)[:48]
            squares = squares + jnp.sum(jnp.square(piece).reshape(6, 8, HALF), axis=0)
        norms.append(jnp.sum(squares, keepdims=True))
    last = keep[0].astype(F32)[48:56]
    mine = lax.axis_index("core")
    last = jnp.where(mine == 0, last, other[0].astype(F32)[48:56])
    norm = norms[0] + norms[1] + jnp.sum(jnp.square(last), keepdims=True)
    factor = jnp.minimum(1.0, clip_norm * lax.rsqrt(norm + 1e-06))
    for half, part in ((mine, keep), (1 - mine, other)):
        for k in range(CHUNKS):
            piece = part[k].astype(F32) * factor
            top = jnp.concatenate([piece[0:16], piece[24:40]], axis=1)
            low = jnp.concatenate([piece[16:24], piece[40:48]], axis=1)
            in_ref[pl.ds(pl.multiple_of(32 * k + 16 * half, 8), 16), :] = top
            out_ref[pl.ds(pl.multiple_of(16 * k + 8 * half, 8), 8), :] = low
    bias_ref[...] = jnp.concatenate([last[0:1], last[1:2]], axis=1) * factor


def shift(value, axis, by, size):
    return lax.ppermute(value, axis, [(i, (i + by) % size) for i in range(size)])


def in_hbm(*values):
    return [pltpu.with_memory_space_constraint(v, pltpu.HBM) for v in values]


def exchange(slots):
    got = [slots[0]]
    got += [shift(slots[d], "sub", d, SUB) for d in range(1, SUB)]
    dom = 1
    for axis in DOM:
        dom *= lax.axis_size(axis)
    return got, dom


def local(feat, cot, vals, src, dst, halo_rows, halo_count, w_in, b_in, w_out):
    block = sds((BLK, H), BF16)
    halves = (CHUNKS, PROWS, HALF)
    by_slot = jnp.transpose(halo_rows, (1, 0, 2))
    slots = pl.pallas_call(
        pick_kernel,
        out_shape=[block] * PEERS,
        in_specs=[HB] * 3,
        out_specs=[VM] * PEERS,
        scratch_shapes=[
            pltpu.VMEM((PEERS, 1, BLK), jnp.int32),
            pltpu.SMEM((1, PEERS), jnp.int32),
            pltpu.VMEM((N, H), BF16),
            pltpu.VMEM((PEERS * BLK, N), BF16),
            pltpu.SemaphoreType.DMA((3,)),
        ],
        compiler_params=params(24),
        name="pick",
    )(*in_hbm(by_slot, halo_count, feat))
    got, dom = exchange(slots)
    got += [shift(slots[4], DOM, 1, dom), shift(slots[5], DOM, -1, dom)]
    near = pl.pallas_call(
        near_kernel,
        out_shape=sds((NB + 1, BLK, H), F32),
        in_specs=[HB] * 4,
        out_specs=VM,
        scratch_shapes=[
            pltpu.SMEM((T,), jnp.int32),
            pltpu.SMEM((T,), jnp.int32),
            pltpu.SMEM((T + NEAR_STEP,), jnp.int32),
            pltpu.VMEM((N, H), BF16),
            pltpu.VMEM((T, BLK, BLK), BF16),
            pltpu.SemaphoreType.DMA((4,)),
        ],
        compiler_params=params(24),
        cost_estimate=pl.CostEstimate(flops=800_000_000, bytes_accessed=6_000_000, transcendentals=0),
        name="near",
    )(*in_hbm(src, dst, feat, vals))
    new_rows, gpre, keep, give = pl.pallas_call(
        node_kernel,
        out_shape=[sds((N, H), BF16), pltpu.HBM((N, H), BF16), sds(halves, F32), sds(halves, BF16)],
        in_specs=[SM, SM] + [VM] * 13,
        out_specs=[HB] * 2 + [VM] * 2,
        scratch_shapes=[
            pltpu.SMEM((T + NEAR_STEP,), jnp.int32),
            pltpu.VMEM((PEERS, BLK, H), BF16),
            pltpu.VMEM((NB + 1, BLK, H), F32),
            pltpu.VMEM((2 * H, H), F32),
            pltpu.VMEM((H, H), F32),
            pltpu.VMEM((N, H), BF16),
            pltpu.VMEM((N, H), BF16),
            pltpu.SemaphoreType.DMA((2, N // CH)),
        ],
        compiler_params=params(32),
        name="node",
    )(src, dst, *got, feat, cot, vals, near, w_in, b_in.reshape(1, H), w_out)
    given = shift(give, "core", 1, 2)
    joined = pl.pallas_call(
        join_kernel, out_shape=sds(halves, BF16), in_specs=[VM] * 2, out_specs=VM, compiler_params=params(4), name="join"
    )(keep, given)
    parts = lax.all_to_all(joined, PLANE, split_axis=0, concat_axis=0, tiled=True)
    own, *slots = pl.pallas_call(
        back_kernel,
        out_shape=[pltpu.HBM((NB, BLK, H), F32)] + [block] * PEERS,
        in_specs=[SM, SM, VM] + [HB] * 3,
        out_specs=[HB] + [VM] * PEERS,
        scratch_shapes=[
            pltpu.VMEM((N, H), BF16),
            pltpu.VMEM((2 * H, H), BF16),
            pltpu.VMEM((N, H), BF16),
            pltpu.VMEM((N, H), BF16),
            pltpu.VMEM((BUF, BLK, H), F32),
            pltpu.SemaphoreType.DMA((4,)),
        ],
        compiler_params=params(20),
        cost_estimate=pl.CostEstimate(flops=4_000_000_000, bytes_accessed=9_000_000, transcendentals=0),
        name="back",
    )(src, dst, vals, *in_hbm(gpre, w_in, cot))
    early, late = (), (1, 2, 3, 4, 5)
    parts, own = lax.optimization_barrier((parts, own))
    depth = lax.axis_size("z")
    paired = pl.pallas_call(
        spread_kernel,
        out_shape=sds((depth, PROWS, HALF), BF16),
        in_specs=[VM],
        out_specs=VM,
        compiler_params=params(4),
        name="fold",
    )(parts)
    got = {0: slots[0]}
    send = {d: (lambda v, d=d: shift(v, "sub", d, SUB)) for d in range(1, SUB)}
    send[4] = lambda v: shift(v, DOM, -1, dom)
    send[5] = lambda v: shift(v, DOM, 1, dom)
    for d in early:
        got[d] = send[d](slots[d])
    held = [slots[d] for d in late]
    paired, *held = lax.optimization_barrier((paired, *held))
    column = lax.all_to_all(paired, "z", split_axis=0, concat_axis=0, tiled=True)
    for d, slot in zip(late, held):
        got[d] = send[d](slot)
    got = [got[d] for d in range(PEERS)]
    column, *got = lax.optimization_barrier((column, *got))
    spread = pl.pallas_call(
        spread_kernel,
        out_shape=sds(halves, BF16),
        in_specs=[VM],
        out_specs=VM,
        compiler_params=params(4),
        name="spread",
    )(column)
    whole = lax.all_to_all(spread, PLANE, split_axis=0, concat_axis=0, tiled=True)
    grad_features = pl.pallas_call(
        land_kernel,
        out_shape=sds((NB, BLK, H), F32),
        in_specs=[HB] * 2 + [VM] * PEERS + [HB],
        out_specs=HB,
        scratch_shapes=[
            pltpu.VMEM((PEERS, 1, BLK), jnp.int32),
            pltpu.SMEM((1, PEERS), jnp.int32),
            pltpu.VMEM((NB, BLK, H), F32),
            pltpu.SemaphoreType.DMA((3 + N // LAND,)),
        ],
        compiler_params=params(20),
        cost_estimate=pl.CostEstimate(flops=5_000_000_000, bytes_accessed=9_000_000, transcendentals=0),
        name="land",
    )(*in_hbm(by_slot, halo_count), *got, *in_hbm(own)).reshape(N, H)
    whole, grad_features = lax.optimization_barrier((whole, grad_features))
    other = shift(whole, "core", 1, 2)
    g_in, g_bias, g_out = pl.pallas_call(
        clip_kernel,
        out_shape=[sds((2 * H, H), F32), sds((1, H), F32), sds((H, H), F32)],
        in_specs=[VM] * 2,
        out_specs=[VM] * 3,
        compiler_params=params(8),
        name="clip",
    )(whole, other)
    return new_rows, grad_features, g_in, g_bias.reshape(H), g_out


def solution(mesh):
    grid = Mesh(mesh.devices.reshape(4, 8, 2, 4), ALL)
    split2, split1 = P(ALL, None), P(ALL)
    split3 = P(ALL, None, None)
    return jax.shard_map(
        local,
        mesh=grid,
        in_specs=(split2, split2, split3, split1, split1, split3, split2, P(), P(), P()),
        out_specs=(split2, split2, P(), P(), P()),
        check_vma=False,
    )
```

```python
import jax
import jax.numpy as jnp
from jax import lax
from jax.experimental import pallas as pl
from jax.experimental.pallas import tpu as pltpu
from jax.sharding import Mesh, PartitionSpec as P

H = 256
BLK = 128
NB = 16
N = NB * BLK
T = 64
PEERS = 6
SUB = 4
BUF = NB + PEERS
CHUNKS = 16
PROWS = 56
HALF = H // 2
CH = 1024
NEAR_STEP = 16
FAR_STEP = 8
BACK = 512
BACK_STEP = 64
LAND = 512
LEGS = ((4, 5), (1, 3), (2,))
clip_norm = 256.0
ln_eps = 1e-05
F32 = jnp.float32
BF16 = jnp.bfloat16
ALL = ("x", "z", "core", "sub")
DOM = ("x", "z", "core")
PLANE = ("x", "sub")
MIB = 1024 * 1024
VM = pl.BlockSpec(memory_space=pltpu.VMEM)
HB = pl.BlockSpec(memory_space=pltpu.HBM)
SM = pl.BlockSpec(memory_space=pltpu.SMEM)


def params(mib):
    return pltpu.CompilerParams(vmem_limit_bytes=mib * MIB)


def sds(shape, dtype):
    return jax.ShapeDtypeStruct(shape, dtype)


def dot(a, b):
    return jnp.dot(a, b, preferred_element_type=F32)


def dot_t0(a, b):
    return lax.dot_general(a, b, (((0,), (0,)), ((), ())), preferred_element_type=F32)


def dot_t1(a, b):
    return lax.dot_general(a, b, (((1,), (1,)), ((), ())), preferred_element_type=F32)


def pick_kernel(rows_hbm, count_hbm, feat_hbm, o0, o1, o2, o3, o4, o5, rows, count, feat, hot, sems):
    load_rows = pltpu.make_async_copy(rows_hbm, rows, sems.at[0])
    load_count = pltpu.make_async_copy(count_hbm, count, sems.at[1])
    load_feat = pltpu.make_async_copy(feat_hbm, feat, sems.at[2])
    load_rows.start()
    load_count.start()
    load_feat.start()
    me = lax.axis_index("sub")
    load_rows.wait()
    load_count.wait()
    lane = lax.broadcasted_iota(jnp.int32, (1, BLK), 1)
    node = lax.broadcasted_iota(jnp.int32, (BLK, N), 1)
    for d in range(PEERS):
        q = lax.rem(me + d, SUB) if d < SUB else d
        ids = jnp.where(lane < count[0, q], rows[q], -1)
        column = jnp.transpose(jnp.broadcast_to(ids, (8, BLK)))[:, :1]
        hot[pl.ds(d * BLK, BLK), :] = jnp.where(node == column, 1.0, 0.0).astype(BF16)
    load_feat.wait()
    picked = dot(hot[...], feat[...]).astype(BF16)
    for d, o in enumerate((o0, o1, o2, o3, o4, o5)):
        o[...] = picked[d * BLK : (d + 1) * BLK]


def list_tiles(src_ref, dst_ref, listed, least, most, spare):
    def step(t, n):
        s = src_ref[t]
        listed[n] = (dst_ref[t] * 32 + s) * 64 + t
        return n + jnp.where((s >= least) & (s < most), 1, 0)

    n = lax.fori_loop(0, T, step, jnp.int32(0), unroll=True)
    for p in range(spare):
        listed[n + p] = (NB * 32 + least) * 64
    return n


def near_kernel(src_hbm, dst_hbm, feat_hbm, vals_hbm, total, src, dst, listed, feat, vals, sems):
    load_src = pltpu.make_async_copy(src_hbm, src, sems.at[0])
    load_dst = pltpu.make_async_copy(dst_hbm, dst, sems.at[1])
    load_feat = pltpu.make_async_copy(feat_hbm, feat, sems.at[2])
    load_vals = pltpu.make_async_copy(vals_hbm, vals, sems.at[3])
    load_src.start()
    load_dst.start()
    load_feat.start()
    load_vals.start()
    total[...] = jnp.zeros_like(total)
    load_src.wait()
    load_dst.wait()
    n = list_tiles(src, dst, listed, 0, NB, NEAR_STEP)
    load_feat.wait()
    load_vals.wait()

    def step(i, _):
        for u in range(NEAR_STEP):
            packed = listed[i * NEAR_STEP + u]
            t, s, d = packed % 64, (packed // 64) % 32, packed // 2048
            rows = feat[pl.ds(pl.multiple_of(s * BLK, BLK), BLK), :]
            total[d] += dot(vals[t], rows)
        return 0

    lax.fori_loop(0, pl.cdiv(n, NEAR_STEP), step, 0)


def node_kernel(
    src_ref, dst_ref, h0, h1, h2, h3, h4, h5, feat_ref, cot_ref, vals_ref, near_ref,
    win_ref, bin_ref, wout_ref, new_hbm, gpre_hbm, keep_ref, give_ref, listed, halo, total, sum_in, sum_out,
    new_rows, grad_pre, sems,
):
    n = list_tiles(src_ref, dst_ref, listed, NB, BUF, FAR_STEP)
    me = lax.axis_index("sub")
    for d, h in enumerate((h0, h1, h2, h3, h4, h5)):
        q = lax.rem(me + SUB - d, SUB) if d < SUB else d
        halo[q] = h[...]
    total[...] = near_ref[...]

    def step(i, _):
        for u in range(FAR_STEP):
            packed = listed[i * FAR_STEP + u]
            t, s, d = packed % 64, (packed // 64) % 32, packed // 2048
            total[d] += dot(vals_ref[t], halo[s - NB])
        return 0

    lax.fori_loop(0, pl.cdiv(n, FAR_STEP), step, 0)
    w_in, b_in, w_out = win_ref[...], bin_ref[...], wout_ref[...]
    sum_bias = jnp.zeros((1, H), F32)
    stores = []
    for c in range(N // CH):
        rows = pl.ds(c * CH, CH)
        per = CH // BLK
        agg = total[pl.ds(c * per, per)].reshape(CH, H).astype(BF16)
        feat = feat_ref[rows, :]
        joined = jnp.concatenate([feat, agg], axis=1)
        pre = dot(joined, w_in) + b_in
        sig = 1.0 / (1.0 + jnp.exp(-pre))
        act = (pre * sig).astype(BF16)
        slope = sig * (1.0 + pre * (1.0 - sig))
        lifted = dot(act, w_out)
        centred = lifted - jnp.mean(lifted, axis=1, keepdims=True)
        inv_std = lax.rsqrt(jnp.mean(centred * centred, axis=1, keepdims=True) + ln_eps)
        normed = centred * inv_std
        new_rows[rows, :] = (feat.astype(F32) + normed).astype(BF16)
        store = pltpu.make_async_copy(new_rows.at[rows, :], new_hbm.at[rows, :], sems.at[0, c])
        store.start()
        stores.append(store)
        up = cot_ref[rows, :].astype(F32)
        grad_lifted = inv_std * (
            up
            - jnp.mean(up, axis=1, keepdims=True)
            - normed * jnp.mean(up * normed, axis=1, keepdims=True)
        )
        grad_lifted = grad_lifted.astype(BF16)
        gpre = (dot_t1(grad_lifted, w_out) * slope).astype(BF16)
        grad_pre[rows, :] = gpre
        store = pltpu.make_async_copy(grad_pre.at[rows, :], gpre_hbm.at[rows, :], sems.at[1, c])
        store.start()
        stores.append(store)
        g_out = dot_t0(act, grad_lifted)
        g_in = dot_t0(joined, gpre)
        sum_bias = sum_bias + jnp.sum(gpre.astype(F32), axis=0, keepdims=True)
        if c == 0:
            sum_in[...] = g_in
            sum_out[...] = g_out
        else:
            sum_in[...] += g_in
            sum_out[...] += g_out
    bias = jnp.concatenate([sum_bias[:, :HALF], sum_bias[:, HALF:], jnp.zeros((6, HALF), F32)], axis=0)
    mine = lax.axis_index("core")
    for half, out in ((mine, keep_ref), (1 - mine, give_ref)):
        for k in range(CHUNKS):
            top = sum_in[pl.ds(pl.multiple_of(32 * k + 16 * half, 8), 16), :]
            low = sum_out[pl.ds(pl.multiple_of(16 * k + 8 * half, 8), 8), :]
            last = bias if k == 0 else jnp.zeros((8, HALF), F32)
            piece = jnp.concatenate(
                [top[:, :HALF], low[:, :HALF], top[:, HALF:], low[:, HALF:], last], axis=0
            )
            out[k] = piece.astype(out.dtype)
    for store in stores:
        store.wait()


def back_kernel(
    src_ref, dst_ref, vals_ref, gpre_hbm, win_hbm, cot_hbm, own_hbm, o0, o1, o2, o3, o4, o5,
    gpre, win, cot, grad_agg, total, sems,
):
    loads = [pltpu.make_async_copy(win_hbm, win, sems.at[0])]
    for c in range(N // BACK):
        rows = pl.ds(c * BACK, BACK)
        loads.append(pltpu.make_async_copy(gpre_hbm.at[rows, :], gpre.at[rows, :], sems.at[2 * c + 1]))
        loads.append(pltpu.make_async_copy(cot_hbm.at[rows, :], cot.at[rows, :], sems.at[2 * c + 2]))
    for load in loads:
        load.start()
    total[pl.ds(NB, PEERS)] = jnp.zeros((PEERS, BLK, H), F32)
    loads[0].wait()
    w_in = win[...]
    per = BACK // BLK
    for c in range(N // BACK):
        rows = pl.ds(c * BACK, BACK)
        loads[2 * c + 1].wait()
        loads[2 * c + 2].wait()
        joined = dot_t1(gpre[rows, :], w_in)
        grad_agg[rows, :] = joined[:, H:].astype(BF16)
        direct = cot[rows, :].astype(F32) + joined[:, :H]
        total[pl.ds(c * per, per)] = direct.reshape(per, BLK, H)

    def step(i, _):
        for u in range(BACK_STEP):
            t = i * BACK_STEP + u
            s, d = src_ref[t], dst_ref[t]
            down = grad_agg[pl.ds(pl.multiple_of(d * BLK, BLK), BLK), :]
            total[s] += dot_t0(vals_ref[t], down)
        return 0

    lax.fori_loop(0, T // BACK_STEP, step, 0)
    store = pltpu.make_async_copy(total.at[pl.ds(0, NB)], own_hbm, sems.at[len(loads)])
    store.start()
    me = lax.axis_index("sub")
    for d, o in enumerate((o0, o1, o2, o3, o4, o5)):
        q = lax.rem(me + d, SUB) if d < SUB else d
        o[...] = total[NB + q].astype(BF16)
    store.wait()


def land_kernel(
    rows_hbm, count_hbm, r0, r1, r2, r3, r4, r5, own_hbm, out_hbm, rows_ref, count, own, sems
):
    loads = [
        pltpu.make_async_copy(rows_hbm, rows_ref, sems.at[0]),
        pltpu.make_async_copy(count_hbm, count, sems.at[1]),
        pltpu.make_async_copy(own_hbm, own, sems.at[2]),
    ]
    for load in loads:
        load.start()
    for load in loads[:2]:
        load.wait()
    me = lax.axis_index("sub")
    lane = lax.broadcasted_iota(jnp.int32, (1, BLK), 1)
    ids = []
    for d in range(PEERS):
        q = lax.rem(me + SUB - d, SUB) if d < SUB else d
        ids.append(jnp.where(lane < count[0, q], rows_ref[q], -1))
    ids = jnp.concatenate(ids, axis=1)
    back = jnp.concatenate([r[...] for r in (r0, r1, r2, r3, r4, r5)], axis=0)
    stores = []
    for c in range(N // LAND):
        node = lax.broadcasted_iota(jnp.int32, (LAND, PEERS * BLK), 0) + c * LAND
        hot = jnp.where(node == ids, 1.0, 0.0).astype(BF16)
        landed = dot(hot, back)
        if c == 0:
            loads[2].wait()
        per = LAND // BLK
        blocks = pl.ds(c * per, per)
        own[blocks] += landed.reshape(per, BLK, H)
        store = pltpu.make_async_copy(own.at[blocks], out_hbm.at[blocks], sems.at[3 + c])
        store.start()
        stores.append(store)
    for store in stores:
        store.wait()


def join_kernel(keep, other, out_ref):
    out_ref[...] = (keep[...] + other[...].astype(F32)).astype(BF16)


def fold_kernel(parts, out_ref):
    out_ref[...] = jnp.sum(parts[...].astype(F32), axis=0)


def add_kernel(mine, other, out_ref):
    out_ref[...] = mine[...] + other[...]


def copy_kernel(*refs):
    half = len(refs) // 2
    for a, b in zip(refs[:half], refs[half:]):
        b[...] = a[...]


def spread_kernel(mine, other, out_ref):
    whole = (mine[...] + other[...]).astype(BF16)
    for i in range(out_ref.shape[0]):
        out_ref[i] = whole


def clip_kernel(keep, other, in_ref, bias_ref, out_ref):
    norms = []
    for part in (keep, other):
        squares = jnp.zeros((8, HALF), F32)
        for k in range(CHUNKS):
            piece = part[k].astype(F32)[:48]
            squares = squares + jnp.sum(jnp.square(piece).reshape(6, 8, HALF), axis=0)
        norms.append(jnp.sum(squares, keepdims=True))
    last = keep[0].astype(F32)[48:56]
    mine = lax.axis_index("core")
    last = jnp.where(mine == 0, last, other[0].astype(F32)[48:56])
    norm = norms[0] + norms[1] + jnp.sum(jnp.square(last), keepdims=True)
    factor = jnp.minimum(1.0, clip_norm * lax.rsqrt(norm + 1e-06))
    for half, part in ((mine, keep), (1 - mine, other)):
        for k in range(CHUNKS):
            piece = part[k].astype(F32) * factor
            top = jnp.concatenate([piece[0:16], piece[24:40]], axis=1)
            low = jnp.concatenate([piece[16:24], piece[40:48]], axis=1)
            in_ref[pl.ds(pl.multiple_of(32 * k + 16 * half, 8), 16), :] = top
            out_ref[pl.ds(pl.multiple_of(16 * k + 8 * half, 8), 8), :] = low
    bias_ref[...] = jnp.concatenate([last[0:1], last[1:2]], axis=1) * factor


def shift(value, axis, by, size):
    return lax.ppermute(value, axis, [(i, (i + by) % size) for i in range(size)])


def in_hbm(*values):
    return [pltpu.with_memory_space_constraint(v, pltpu.HBM) for v in values]


def exchange(slots):
    got = [slots[0]]
    got += [shift(slots[d], "sub", d, SUB) for d in range(1, SUB)]
    dom = 1
    for axis in DOM:
        dom *= lax.axis_size(axis)
    return got, dom


def local(feat, cot, vals, src, dst, halo_rows, halo_count, w_in, b_in, w_out):
    block = sds((BLK, H), BF16)
    halves = (CHUNKS, PROWS, HALF)
    by_slot = jnp.transpose(halo_rows, (1, 0, 2))
    slots = pl.pallas_call(
        pick_kernel,
        out_shape=[block] * PEERS,
        in_specs=[HB] * 3,
        out_specs=[VM] * PEERS,
        scratch_shapes=[
            pltpu.VMEM((PEERS, 1, BLK), jnp.int32),
            pltpu.SMEM((1, PEERS), jnp.int32),
            pltpu.VMEM((N, H), BF16),
            pltpu.VMEM((PEERS * BLK, N), BF16),
            pltpu.SemaphoreType.DMA((3,)),
        ],
        compiler_params=params(24),
        name="pick",
    )(*in_hbm(by_slot, halo_count, feat))
    got, dom = exchange(slots)
    got += [shift(slots[4], DOM, 1, dom), shift(slots[5], DOM, -1, dom)]
    near = pl.pallas_call(
        near_kernel,
        out_shape=sds((NB + 1, BLK, H), F32),
        in_specs=[HB] * 4,
        out_specs=VM,
        scratch_shapes=[
            pltpu.SMEM((T,), jnp.int32),
            pltpu.SMEM((T,), jnp.int32),
            pltpu.SMEM((T + NEAR_STEP,), jnp.int32),
            pltpu.VMEM((N, H), BF16),
            pltpu.VMEM((T, BLK, BLK), BF16),
            pltpu.SemaphoreType.DMA((4,)),
        ],
        compiler_params=params(24),
        cost_estimate=pl.CostEstimate(flops=800_000_000, bytes_accessed=6_000_000, transcendentals=0),
        name="near",
    )(*in_hbm(src, dst, feat, vals))
    new_rows, gpre, keep, give = pl.pallas_call(
        node_kernel,
        out_shape=[sds((N, H), BF16), pltpu.HBM((N, H), BF16), sds(halves, F32), sds(halves, BF16)],
        in_specs=[SM, SM] + [VM] * 13,
        out_specs=[HB] * 2 + [VM] * 2,
        scratch_shapes=[
            pltpu.SMEM((T + NEAR_STEP,), jnp.int32),
            pltpu.VMEM((PEERS, BLK, H), BF16),
            pltpu.VMEM((NB + 1, BLK, H), F32),
            pltpu.VMEM((2 * H, H), F32),
            pltpu.VMEM((H, H), F32),
            pltpu.VMEM((N, H), BF16),
            pltpu.VMEM((N, H), BF16),
            pltpu.SemaphoreType.DMA((2, N // CH)),
        ],
        compiler_params=params(32),
        name="node",
    )(src, dst, *got, feat, cot, vals, near, w_in, b_in.reshape(1, H), w_out)
    given = shift(give, "core", 1, 2)
    joined = pl.pallas_call(
        join_kernel, out_shape=sds(halves, BF16), in_specs=[VM] * 2, out_specs=VM, compiler_params=params(4), name="join"
    )(keep, given)
    parts = lax.all_to_all(joined, PLANE, split_axis=0, concat_axis=0, tiled=True)
    own, *slots = pl.pallas_call(
        back_kernel,
        out_shape=[pltpu.HBM((NB, BLK, H), F32)] + [block] * PEERS,
        in_specs=[SM, SM, VM] + [HB] * 3,
        out_specs=[HB] + [VM] * PEERS,
        scratch_shapes=[
            pltpu.VMEM((N, H), BF16),
            pltpu.VMEM((2 * H, H), BF16),
            pltpu.VMEM((N, H), BF16),
            pltpu.VMEM((N, H), BF16),
            pltpu.VMEM((BUF, BLK, H), F32),
            pltpu.SemaphoreType.DMA((2 + 2 * (N // BACK),)),
        ],
        compiler_params=params(20),
        cost_estimate=pl.CostEstimate(flops=4_000_000_000, bytes_accessed=9_000_000, transcendentals=0),
        name="back",
    )(src, dst, vals, *in_hbm(gpre, w_in, cot))
    parts, own = lax.optimization_barrier((parts, own))
    piece = sds((PROWS, HALF), F32)
    part = pl.pallas_call(
        fold_kernel, out_shape=piece, in_specs=[VM], out_specs=VM, compiler_params=params(4), name="fold"
    )(parts)
    depth = lax.axis_size("z")
    send = {d: (lambda v, d=d: shift(v, "sub", d, SUB)) for d in range(1, SUB)}
    send[4] = lambda v: shift(v, DOM, -1, dom)
    send[5] = lambda v: shift(v, DOM, 1, dom)
    got = {0: slots[0]}
    for reach, now in zip((1, 2, 4), LEGS):
        part, *held = lax.optimization_barrier((part, *[slots[d] for d in now]))
        other = lax.ppermute(part, "z", [(i, i ^ reach) for i in range(depth)])
        for d, slot in zip(now, held):
            got[d] = send[d](slot)
        ready = {1: (), 2: (), 4: (4, 5)}[reach]
        other, *back = lax.optimization_barrier((other, *[got[d] for d in ready]))
        for d, slot in zip(ready, back):
            got[d] = slot
        if reach < 4:
            part = pl.pallas_call(
                add_kernel, out_shape=piece, in_specs=[VM] * 2, out_specs=VM, compiler_params=params(4), name="add"
            )(part, other)
    got = [got[d] for d in range(PEERS)]
    spread = pl.pallas_call(
        spread_kernel,
        out_shape=sds(halves, BF16),
        in_specs=[VM] * 2,
        out_specs=VM,
        compiler_params=params(4),
        name="spread",
    )(part, other)
    whole = lax.all_to_all(spread, PLANE, split_axis=0, concat_axis=0, tiled=True)
    grad_features = pl.pallas_call(
        land_kernel,
        out_shape=sds((NB, BLK, H), F32),
        in_specs=[HB] * 2 + [VM] * PEERS + [HB],
        out_specs=HB,
        scratch_shapes=[
            pltpu.VMEM((PEERS, 1, BLK), jnp.int32),
            pltpu.SMEM((1, PEERS), jnp.int32),
            pltpu.VMEM((NB, BLK, H), F32),
            pltpu.SemaphoreType.DMA((3 + N // LAND,)),
        ],
        compiler_params=params(20),
        cost_estimate=pl.CostEstimate(flops=5_000_000_000, bytes_accessed=9_000_000, transcendentals=0),
        name="land",
    )(*in_hbm(by_slot, halo_count), *got, *in_hbm(own)).reshape(N, H)
    whole, grad_features = lax.optimization_barrier((whole, grad_features))
    other = shift(whole, "core", 1, 2)
    g_in, g_bias, g_out = pl.pallas_call(
        clip_kernel,
        out_shape=[sds((2 * H, H), F32), sds((1, H), F32), sds((H, H), F32)],
        in_specs=[VM] * 2,
        out_specs=[VM] * 3,
        compiler_params=params(8),
        name="clip",
    )(whole, other)
    return new_rows, grad_features, g_in, g_bias.reshape(H), g_out


def solution(mesh):
    grid = Mesh(mesh.devices.reshape(4, 8, 2, 4), ALL)
    split2, split1 = P(ALL, None), P(ALL)
    split3 = P(ALL, None, None)
    return jax.shard_map(
        local,
        mesh=grid,
        in_specs=(split2, split2, split3, split1, split1, split3, split2, P(), P(), P()),
        out_specs=(split2, split2, P(), P(), P()),
        check_vma=False,
    )
```

```python
import jax
import jax.numpy as jnp
from jax import lax
from jax.experimental import pallas as pl
from jax.experimental.pallas import tpu as pltpu
from jax.sharding import Mesh, PartitionSpec as P

H = 256
BLK = 128
NB = 16
N = NB * BLK
T = 64
PEERS = 6
SUB = 4
BUF = NB + PEERS
CHUNKS = 16
PROWS = 56
HALF = H // 2
CH = 1024
NEAR_STEP = 16
FAR_STEP = 8
BACK = 512
BACK_STEP = 64
LAND = 512
clip_norm = 256.0
ln_eps = 1e-05
F32 = jnp.float32
BF16 = jnp.bfloat16
ALL = ("x", "z", "core", "sub")
DOM = ("x", "z", "core")
PLANE = ("x", "sub")
MIB = 1024 * 1024
VM = pl.BlockSpec(memory_space=pltpu.VMEM)
HB = pl.BlockSpec(memory_space=pltpu.HBM)
SM = pl.BlockSpec(memory_space=pltpu.SMEM)


def params(mib):
    return pltpu.CompilerParams(vmem_limit_bytes=mib * MIB)


def sds(shape, dtype):
    return jax.ShapeDtypeStruct(shape, dtype)


def dot(a, b):
    return jnp.dot(a, b, preferred_element_type=F32)


def dot_t0(a, b):
    return lax.dot_general(a, b, (((0,), (0,)), ((), ())), preferred_element_type=F32)


def dot_t1(a, b):
    return lax.dot_general(a, b, (((1,), (1,)), ((), ())), preferred_element_type=F32)


def pick_kernel(rows_hbm, count_hbm, feat_hbm, o0, o1, o2, o3, o4, o5, rows, count, feat, hot, sems):
    load_rows = pltpu.make_async_copy(rows_hbm, rows, sems.at[0])
    load_count = pltpu.make_async_copy(count_hbm, count, sems.at[1])
    load_feat = pltpu.make_async_copy(feat_hbm, feat, sems.at[2])
    load_rows.start()
    load_count.start()
    load_feat.start()
    me = lax.axis_index("sub")
    load_rows.wait()
    load_count.wait()
    lane = lax.broadcasted_iota(jnp.int32, (1, BLK), 1)
    node = lax.broadcasted_iota(jnp.int32, (BLK, N), 1)
    for d in range(PEERS):
        q = lax.rem(me + d, SUB) if d < SUB else d
        ids = jnp.where(lane < count[0, q], rows[q], -1)
        column = jnp.transpose(jnp.broadcast_to(ids, (8, BLK)))[:, :1]
        hot[pl.ds(d * BLK, BLK), :] = jnp.where(node == column, 1.0, 0.0).astype(BF16)
    load_feat.wait()
    picked = dot(hot[...], feat[...]).astype(BF16)
    for d, o in enumerate((o0, o1, o2, o3, o4, o5)):
        o[...] = picked[d * BLK : (d + 1) * BLK]


def list_tiles(src_ref, dst_ref, listed, least, most, spare):
    def step(t, n):
        s = src_ref[t]
        listed[n] = (dst_ref[t] * 32 + s) * 64 + t
        return n + jnp.where((s >= least) & (s < most), 1, 0)

    n = lax.fori_loop(0, T, step, jnp.int32(0), unroll=True)
    for p in range(spare):
        listed[n + p] = (NB * 32 + least) * 64
    return n


def near_kernel(src_hbm, dst_hbm, feat_hbm, vals_hbm, total, src, dst, listed, feat, vals, sems):
    load_src = pltpu.make_async_copy(src_hbm, src, sems.at[0])
    load_dst = pltpu.make_async_copy(dst_hbm, dst, sems.at[1])
    load_feat = pltpu.make_async_copy(feat_hbm, feat, sems.at[2])
    load_vals = pltpu.make_async_copy(vals_hbm, vals, sems.at[3])
    load_src.start()
    load_dst.start()
    load_feat.start()
    load_vals.start()
    total[...] = jnp.zeros_like(total)
    load_src.wait()
    load_dst.wait()
    n = list_tiles(src, dst, listed, 0, NB, NEAR_STEP)
    load_feat.wait()
    load_vals.wait()

    def step(i, _):
        for u in range(NEAR_STEP):
            packed = listed[i * NEAR_STEP + u]
            t, s, d = packed % 64, (packed // 64) % 32, packed // 2048
            rows = feat[pl.ds(pl.multiple_of(s * BLK, BLK), BLK), :]
            total[d] += dot(vals[t], rows)
        return 0

    lax.fori_loop(0, pl.cdiv(n, NEAR_STEP), step, 0)


def node_kernel(
    src_ref, dst_ref, h0, h1, h2, h3, h4, h5, feat_ref, cot_ref, vals_ref, near_ref,
    win_ref, bin_ref, wout_ref, new_hbm, gpre_hbm, keep_ref, give_ref, listed, halo, total, sum_in, sum_out,
    new_rows, grad_pre, sems,
):
    n = list_tiles(src_ref, dst_ref, listed, NB, BUF, FAR_STEP)
    me = lax.axis_index("sub")
    for d, h in enumerate((h0, h1, h2, h3, h4, h5)):
        q = lax.rem(me + SUB - d, SUB) if d < SUB else d
        halo[q] = h[...]
    total[...] = near_ref[...]

    def step(i, _):
        for u in range(FAR_STEP):
            packed = listed[i * FAR_STEP + u]
            t, s, d = packed % 64, (packed // 64) % 32, packed // 2048
            total[d] += dot(vals_ref[t], halo[s - NB])
        return 0

    lax.fori_loop(0, pl.cdiv(n, FAR_STEP), step, 0)
    w_in, b_in, w_out = win_ref[...], bin_ref[...], wout_ref[...]
    sum_bias = jnp.zeros((1, H), F32)
    stores = []
    for c in range(N // CH):
        rows = pl.ds(c * CH, CH)
        per = CH // BLK
        agg = total[pl.ds(c * per, per)].reshape(CH, H).astype(BF16)
        feat = feat_ref[rows, :]
        joined = jnp.concatenate([feat, agg], axis=1)
        pre = dot(joined, w_in) + b_in
        sig = 1.0 / (1.0 + jnp.exp(-pre))
        act = (pre * sig).astype(BF16)
        slope = sig * (1.0 + pre * (1.0 - sig))
        lifted = dot(act, w_out)
        centred = lifted - jnp.mean(lifted, axis=1, keepdims=True)
        inv_std = lax.rsqrt(jnp.mean(centred * centred, axis=1, keepdims=True) + ln_eps)
        normed = centred * inv_std
        new_rows[rows, :] = (feat.astype(F32) + normed).astype(BF16)
        store = pltpu.make_async_copy(new_rows.at[rows, :], new_hbm.at[rows, :], sems.at[0, c])
        store.start()
        stores.append(store)
        up = cot_ref[rows, :].astype(F32)
        grad_lifted = inv_std * (
            up
            - jnp.mean(up, axis=1, keepdims=True)
            - normed * jnp.mean(up * normed, axis=1, keepdims=True)
        )
        grad_lifted = grad_lifted.astype(BF16)
        gpre = (dot_t1(grad_lifted, w_out) * slope).astype(BF16)
        grad_pre[rows, :] = gpre
        store = pltpu.make_async_copy(grad_pre.at[rows, :], gpre_hbm.at[rows, :], sems.at[1, c])
        store.start()
        stores.append(store)
        g_out = dot_t0(act, grad_lifted)
        g_in = dot_t0(joined, gpre)
        sum_bias = sum_bias + jnp.sum(gpre.astype(F32), axis=0, keepdims=True)
        if c == 0:
            sum_in[...] = g_in
            sum_out[...] = g_out
        else:
            sum_in[...] += g_in
            sum_out[...] += g_out
    bias = jnp.concatenate([sum_bias[:, :HALF], sum_bias[:, HALF:], jnp.zeros((6, HALF), F32)], axis=0)
    mine = lax.axis_index("core")
    for half, out in ((mine, keep_ref), (1 - mine, give_ref)):
        for k in range(CHUNKS):
            top = sum_in[pl.ds(pl.multiple_of(32 * k + 16 * half, 8), 16), :]
            low = sum_out[pl.ds(pl.multiple_of(16 * k + 8 * half, 8), 8), :]
            last = bias if k == 0 else jnp.zeros((8, HALF), F32)
            piece = jnp.concatenate(
                [top[:, :HALF], low[:, :HALF], top[:, HALF:], low[:, HALF:], last], axis=0
            )
            out[k] = piece.astype(out.dtype)
    for store in stores:
        store.wait()


def back_kernel(
    src_ref, dst_ref, vals_ref, gpre_hbm, win_hbm, cot_hbm, own_hbm, o0, o1, o2, o3, o4, o5,
    gpre, win, cot, grad_agg, total, sems,
):
    loads = [
        pltpu.make_async_copy(win_hbm, win, sems.at[0]),
        pltpu.make_async_copy(gpre_hbm, gpre, sems.at[1]),
        pltpu.make_async_copy(cot_hbm, cot, sems.at[2]),
    ]
    for load in loads:
        load.start()
    total[pl.ds(NB, PEERS)] = jnp.zeros((PEERS, BLK, H), F32)
    for load in loads:
        load.wait()
    w_in = win[...]
    per = BACK // BLK
    for c in range(N // BACK):
        rows = pl.ds(c * BACK, BACK)
        joined = dot_t1(gpre[rows, :], w_in)
        grad_agg[rows, :] = joined[:, H:].astype(BF16)
        direct = cot[rows, :].astype(F32) + joined[:, :H]
        total[pl.ds(c * per, per)] = direct.reshape(per, BLK, H)

    def step(i, _):
        for u in range(BACK_STEP):
            t = i * BACK_STEP + u
            s, d = src_ref[t], dst_ref[t]
            down = grad_agg[pl.ds(pl.multiple_of(d * BLK, BLK), BLK), :]
            total[s] += dot_t0(vals_ref[t], down)
        return 0

    lax.fori_loop(0, T // BACK_STEP, step, 0)
    store = pltpu.make_async_copy(total.at[pl.ds(0, NB)], own_hbm, sems.at[3])
    store.start()
    me = lax.axis_index("sub")
    for d, o in enumerate((o0, o1, o2, o3, o4, o5)):
        q = lax.rem(me + d, SUB) if d < SUB else d
        o[...] = total[NB + q].astype(BF16)
    store.wait()


def land_kernel(
    rows_hbm, count_hbm, r0, r1, r2, r3, r4, r5, own_hbm, out_hbm, rows_ref, count, own, sems
):
    loads = [
        pltpu.make_async_copy(rows_hbm, rows_ref, sems.at[0]),
        pltpu.make_async_copy(count_hbm, count, sems.at[1]),
        pltpu.make_async_copy(own_hbm, own, sems.at[2]),
    ]
    for load in loads:
        load.start()
    for load in loads[:2]:
        load.wait()
    me = lax.axis_index("sub")
    lane = lax.broadcasted_iota(jnp.int32, (1, BLK), 1)
    ids = []
    for d in range(PEERS):
        q = lax.rem(me + SUB - d, SUB) if d < SUB else d
        ids.append(jnp.where(lane < count[0, q], rows_ref[q], -1))
    ids = jnp.concatenate(ids, axis=1)
    back = jnp.concatenate([r[...] for r in (r0, r1, r2, r3, r4, r5)], axis=0)
    stores = []
    for c in range(N // LAND):
        node = lax.broadcasted_iota(jnp.int32, (LAND, PEERS * BLK), 0) + c * LAND
        hot = jnp.where(node == ids, 1.0, 0.0).astype(BF16)
        landed = dot(hot, back)
        if c == 0:
            loads[2].wait()
        per = LAND // BLK
        blocks = pl.ds(c * per, per)
        own[blocks] += landed.reshape(per, BLK, H)
        store = pltpu.make_async_copy(own.at[blocks], out_hbm.at[blocks], sems.at[3 + c])
        store.start()
        stores.append(store)
    for store in stores:
        store.wait()


def join_kernel(keep, other, out_ref):
    out_ref[...] = (keep[...] + other[...].astype(F32)).astype(BF16)


def spread_kernel(parts, out_ref):
    whole = jnp.sum(parts[...].astype(F32), axis=0).astype(BF16)
    for i in range(out_ref.shape[0]):
        out_ref[i] = whole


def clip_kernel(keep, other, in_ref, bias_ref, out_ref):
    norms = []
    for part in (keep, other):
        squares = jnp.zeros((8, HALF), F32)
        for k in range(CHUNKS):
            piece = part[k].astype(F32)[:48]
            squares = squares + jnp.sum(jnp.square(piece).reshape(6, 8, HALF), axis=0)
        norms.append(jnp.sum(squares, keepdims=True))
    last = keep[0].astype(F32)[48:56]
    mine = lax.axis_index("core")
    last = jnp.where(mine == 0, last, other[0].astype(F32)[48:56])
    norm = norms[0] + norms[1] + jnp.sum(jnp.square(last), keepdims=True)
    factor = jnp.minimum(1.0, clip_norm * lax.rsqrt(norm + 1e-06))
    for half, part in ((mine, keep), (1 - mine, other)):
        for k in range(CHUNKS):
            piece = part[k].astype(F32) * factor
            top = jnp.concatenate([piece[0:16], piece[24:40]], axis=1)
            low = jnp.concatenate([piece[16:24], piece[40:48]], axis=1)
            in_ref[pl.ds(pl.multiple_of(32 * k + 16 * half, 8), 16), :] = top
            out_ref[pl.ds(pl.multiple_of(16 * k + 8 * half, 8), 8), :] = low
    bias_ref[...] = jnp.concatenate([last[0:1], last[1:2]], axis=1) * factor


def shift(value, axis, by, size):
    return lax.ppermute(value, axis, [(i, (i + by) % size) for i in range(size)])


def in_hbm(*values):
    return [pltpu.with_memory_space_constraint(v, pltpu.HBM) for v in values]


def exchange(slots):
    got = [slots[0]]
    got += [shift(slots[d], "sub", d, SUB) for d in range(1, SUB)]
    dom = 1
    for axis in DOM:
        dom *= lax.axis_size(axis)
    return got, dom


def local(feat, cot, vals, src, dst, halo_rows, halo_count, w_in, b_in, w_out):
    block = sds((BLK, H), BF16)
    halves = (CHUNKS, PROWS, HALF)
    by_slot = jnp.transpose(halo_rows, (1, 0, 2))
    slots = pl.pallas_call(
        pick_kernel,
        out_shape=[block] * PEERS,
        in_specs=[HB] * 3,
        out_specs=[VM] * PEERS,
        scratch_shapes=[
            pltpu.VMEM((PEERS, 1, BLK), jnp.int32),
            pltpu.SMEM((1, PEERS), jnp.int32),
            pltpu.VMEM((N, H), BF16),
            pltpu.VMEM((PEERS * BLK, N), BF16),
            pltpu.SemaphoreType.DMA((3,)),
        ],
        compiler_params=params(24),
        name="pick",
    )(*in_hbm(by_slot, halo_count, feat))
    got, dom = exchange(slots)
    got += [shift(slots[4], DOM, 1, dom), shift(slots[5], DOM, -1, dom)]
    near = pl.pallas_call(
        near_kernel,
        out_shape=sds((NB + 1, BLK, H), F32),
        in_specs=[HB] * 4,
        out_specs=VM,
        scratch_shapes=[
            pltpu.SMEM((T,), jnp.int32),
            pltpu.SMEM((T,), jnp.int32),
            pltpu.SMEM((T + NEAR_STEP,), jnp.int32),
            pltpu.VMEM((N, H), BF16),
            pltpu.VMEM((T, BLK, BLK), BF16),
            pltpu.SemaphoreType.DMA((4,)),
        ],
        compiler_params=params(24),
        cost_estimate=pl.CostEstimate(flops=800_000_000, bytes_accessed=6_000_000, transcendentals=0),
        name="near",
    )(*in_hbm(src, dst, feat, vals))
    new_rows, gpre, keep, give = pl.pallas_call(
        node_kernel,
        out_shape=[sds((N, H), BF16), pltpu.HBM((N, H), BF16), sds(halves, F32), sds(halves, BF16)],
        in_specs=[SM, SM] + [VM] * 13,
        out_specs=[HB] * 2 + [VM] * 2,
        scratch_shapes=[
            pltpu.SMEM((T + NEAR_STEP,), jnp.int32),
            pltpu.VMEM((PEERS, BLK, H), BF16),
            pltpu.VMEM((NB + 1, BLK, H), F32),
            pltpu.VMEM((2 * H, H), F32),
            pltpu.VMEM((H, H), F32),
            pltpu.VMEM((N, H), BF16),
            pltpu.VMEM((N, H), BF16),
            pltpu.SemaphoreType.DMA((2, N // CH)),
        ],
        compiler_params=params(32),
        name="node",
    )(src, dst, *got, feat, cot, vals, near, w_in, b_in.reshape(1, H), w_out)
    given = shift(give, "core", 1, 2)
    joined = pl.pallas_call(
        join_kernel, out_shape=sds(halves, BF16), in_specs=[VM] * 2, out_specs=VM, compiler_params=params(4), name="join"
    )(keep, given)
    parts = lax.all_to_all(joined, PLANE, split_axis=0, concat_axis=0, tiled=True)
    own, *slots = pl.pallas_call(
        back_kernel,
        out_shape=[pltpu.HBM((NB, BLK, H), F32)] + [block] * PEERS,
        in_specs=[SM, SM, VM] + [HB] * 3,
        out_specs=[HB] + [VM] * PEERS,
        scratch_shapes=[
            pltpu.VMEM((N, H), BF16),
            pltpu.VMEM((2 * H, H), BF16),
            pltpu.VMEM((N, H), BF16),
            pltpu.VMEM((N, H), BF16),
            pltpu.VMEM((BUF, BLK, H), F32),
            pltpu.SemaphoreType.DMA((4,)),
        ],
        compiler_params=params(20),
        cost_estimate=pl.CostEstimate(flops=4_000_000_000, bytes_accessed=9_000_000, transcendentals=0),
        name="back",
    )(src, dst, vals, *in_hbm(gpre, w_in, cot))
    parts, own = lax.optimization_barrier((parts, own))
    depth = lax.axis_size("z")
    paired = pl.pallas_call(
        spread_kernel,
        out_shape=sds((depth, PROWS, HALF), BF16),
        in_specs=[VM],
        out_specs=VM,
        compiler_params=params(4),
        name="fold",
    )(parts)
    paired, *slots[1:SUB] = lax.optimization_barrier((paired, *slots[1:SUB]))
    column = lax.all_to_all(paired, "z", split_axis=0, concat_axis=0, tiled=True)
    got = [slots[0]] + [shift(slots[d], "sub", d, SUB) for d in range(1, SUB)]
    column, *got[1:] = lax.optimization_barrier((column, *got[1:]))
    spread = pl.pallas_call(
        spread_kernel,
        out_shape=sds(halves, BF16),
        in_specs=[VM],
        out_specs=VM,
        compiler_params=params(4),
        name="spread",
    )(column)
    spread, *far = lax.optimization_barrier((spread, *slots[SUB:]))
    whole = lax.all_to_all(spread, PLANE, split_axis=0, concat_axis=0, tiled=True)
    got += [shift(far[0], DOM, -1, dom), shift(far[1], DOM, 1, dom)]
    grad_features = pl.pallas_call(
        land_kernel,
        out_shape=sds((NB, BLK, H), F32),
        in_specs=[HB] * 2 + [VM] * PEERS + [HB],
        out_specs=HB,
        scratch_shapes=[
            pltpu.VMEM((PEERS, 1, BLK), jnp.int32),
            pltpu.SMEM((1, PEERS), jnp.int32),
            pltpu.VMEM((NB, BLK, H), F32),
            pltpu.SemaphoreType.DMA((3 + N // LAND,)),
        ],
        compiler_params=params(20),
        cost_estimate=pl.CostEstimate(flops=5_000_000_000, bytes_accessed=9_000_000, transcendentals=0),
        name="land",
    )(*in_hbm(by_slot, halo_count), *got, *in_hbm(own)).reshape(N, H)
    whole, grad_features = lax.optimization_barrier((whole, grad_features))
    other = shift(whole, "core", 1, 2)
    g_in, g_bias, g_out = pl.pallas_call(
        clip_kernel,
        out_shape=[sds((2 * H, H), F32), sds((1, H), F32), sds((H, H), F32)],
        in_specs=[VM] * 2,
        out_specs=[VM] * 3,
        compiler_params=params(8),
        name="clip",
    )(whole, other)
    return new_rows, grad_features, g_in, g_bias.reshape(H), g_out


def solution(mesh):
    grid = Mesh(mesh.devices.reshape(4, 8, 2, 4), ALL)
    split2, split1 = P(ALL, None), P(ALL)
    split3 = P(ALL, None, None)
    return jax.shard_map(
        local,
        mesh=grid,
        in_specs=(split2, split2, split3, split1, split1, split3, split2, P(), P(), P()),
        out_specs=(split2, split2, P(), P(), P()),
        check_vma=False,
    )
```

```python
import jax
import jax.numpy as jnp
from jax import lax
from jax.experimental import pallas as pl
from jax.experimental.pallas import tpu as pltpu
from jax.sharding import Mesh, PartitionSpec as P

H = 256
BLK = 128
NB = 16
N = NB * BLK
T = 64
PEERS = 6
SUB = 4
BUF = NB + PEERS
CHUNKS = 16
PROWS = 56
HALF = H // 2
CH = 1024
NEAR_STEP = 16
FAR_STEP = 8
BACK = 512
BACK_STEP = 64
LAND = 512
clip_norm = 256.0
ln_eps = 1e-05
F32 = jnp.float32
BF16 = jnp.bfloat16
ALL = ("x", "z", "core", "sub")
DOM = ("x", "z", "core")
PLANE = ("x", "sub")
MIB = 1024 * 1024
VM = pl.BlockSpec(memory_space=pltpu.VMEM)
HB = pl.BlockSpec(memory_space=pltpu.HBM)
SM = pl.BlockSpec(memory_space=pltpu.SMEM)


def params(mib):
    return pltpu.CompilerParams(vmem_limit_bytes=mib * MIB)


def sds(shape, dtype):
    return jax.ShapeDtypeStruct(shape, dtype)


def dot(a, b):
    return jnp.dot(a, b, preferred_element_type=F32)


def dot_t0(a, b):
    return lax.dot_general(a, b, (((0,), (0,)), ((), ())), preferred_element_type=F32)


def dot_t1(a, b):
    return lax.dot_general(a, b, (((1,), (1,)), ((), ())), preferred_element_type=F32)


def pick_kernel(rows_hbm, count_hbm, feat_hbm, o0, o1, o2, o3, o4, o5, rows, count, feat, hot, sems):
    load_rows = pltpu.make_async_copy(rows_hbm, rows, sems.at[0])
    load_count = pltpu.make_async_copy(count_hbm, count, sems.at[1])
    load_feat = pltpu.make_async_copy(feat_hbm, feat, sems.at[2])
    load_rows.start()
    load_count.start()
    load_feat.start()
    me = lax.axis_index("sub")
    load_rows.wait()
    load_count.wait()
    lane = lax.broadcasted_iota(jnp.int32, (1, BLK), 1)
    node = lax.broadcasted_iota(jnp.int32, (BLK, N), 1)
    for d in range(PEERS):
        q = lax.rem(me + d, SUB) if d < SUB else d
        ids = jnp.where(lane < count[0, q], rows[q], -1)
        column = jnp.transpose(jnp.broadcast_to(ids, (8, BLK)))[:, :1]
        hot[pl.ds(d * BLK, BLK), :] = jnp.where(node == column, 1.0, 0.0).astype(BF16)
    load_feat.wait()
    picked = dot(hot[...], feat[...]).astype(BF16)
    for d, o in enumerate((o0, o1, o2, o3, o4, o5)):
        o[...] = picked[d * BLK : (d + 1) * BLK]


def list_tiles(src_ref, dst_ref, listed, least, most, spare):
    def step(t, n):
        s = src_ref[t]
        listed[n] = (dst_ref[t] * 32 + s) * 64 + t
        return n + jnp.where((s >= least) & (s < most), 1, 0)

    n = lax.fori_loop(0, T, step, jnp.int32(0), unroll=True)
    for p in range(spare):
        listed[n + p] = (NB * 32 + least) * 64
    return n


def near_kernel(src_hbm, dst_hbm, feat_hbm, vals_hbm, total, src, dst, listed, feat, vals, sems):
    load_src = pltpu.make_async_copy(src_hbm, src, sems.at[0])
    load_dst = pltpu.make_async_copy(dst_hbm, dst, sems.at[1])
    load_feat = pltpu.make_async_copy(feat_hbm, feat, sems.at[2])
    load_vals = pltpu.make_async_copy(vals_hbm, vals, sems.at[3])
    load_src.start()
    load_dst.start()
    load_feat.start()
    load_vals.start()
    total[...] = jnp.zeros_like(total)
    load_src.wait()
    load_dst.wait()
    n = list_tiles(src, dst, listed, 0, NB, NEAR_STEP)
    load_feat.wait()
    load_vals.wait()

    def step(i, _):
        for u in range(NEAR_STEP):
            packed = listed[i * NEAR_STEP + u]
            t, s, d = packed % 64, (packed // 64) % 32, packed // 2048
            rows = feat[pl.ds(pl.multiple_of(s * BLK, BLK), BLK), :]
            total[d] += dot(vals[t], rows)
        return 0

    lax.fori_loop(0, pl.cdiv(n, NEAR_STEP), step, 0)


def node_kernel(
    src_ref, dst_ref, h0, h1, h2, h3, h4, h5, feat_ref, cot_ref, vals_ref, near_ref,
    win_ref, bin_ref, wout_ref, new_hbm, gpre_hbm, keep_ref, give_ref, listed, halo, total, sum_in, sum_out,
    new_rows, grad_pre, sems,
):
    n = list_tiles(src_ref, dst_ref, listed, NB, BUF, FAR_STEP)
    me = lax.axis_index("sub")
    for d, h in enumerate((h0, h1, h2, h3, h4, h5)):
        q = lax.rem(me + SUB - d, SUB) if d < SUB else d
        halo[q] = h[...]
    total[...] = near_ref[...]

    def step(i, _):
        for u in range(FAR_STEP):
            packed = listed[i * FAR_STEP + u]
            t, s, d = packed % 64, (packed // 64) % 32, packed // 2048
            total[d] += dot(vals_ref[t], halo[s - NB])
        return 0

    lax.fori_loop(0, pl.cdiv(n, FAR_STEP), step, 0)
    w_in, b_in, w_out = win_ref[...], bin_ref[...], wout_ref[...]
    sum_bias = jnp.zeros((1, H), F32)
    stores = []
    for c in range(N // CH):
        rows = pl.ds(c * CH, CH)
        per = CH // BLK
        agg = total[pl.ds(c * per, per)].reshape(CH, H).astype(BF16)
        feat = feat_ref[rows, :]
        joined = jnp.concatenate([feat, agg], axis=1)
        pre = dot(joined, w_in) + b_in
        sig = 1.0 / (1.0 + jnp.exp(-pre))
        act = (pre * sig).astype(BF16)
        slope = sig * (1.0 + pre * (1.0 - sig))
        lifted = dot(act, w_out)
        centred = lifted - jnp.mean(lifted, axis=1, keepdims=True)
        inv_std = lax.rsqrt(jnp.mean(centred * centred, axis=1, keepdims=True) + ln_eps)
        normed = centred * inv_std
        new_rows[rows, :] = (feat.astype(F32) + normed).astype(BF16)
        store = pltpu.make_async_copy(new_rows.at[rows, :], new_hbm.at[rows, :], sems.at[0, c])
        store.start()
        stores.append(store)
        up = cot_ref[rows, :].astype(F32)
        grad_lifted = inv_std * (
            up
            - jnp.mean(up, axis=1, keepdims=True)
            - normed * jnp.mean(up * normed, axis=1, keepdims=True)
        )
        grad_lifted = grad_lifted.astype(BF16)
        gpre = (dot_t1(grad_lifted, w_out) * slope).astype(BF16)
        grad_pre[rows, :] = gpre
        store = pltpu.make_async_copy(grad_pre.at[rows, :], gpre_hbm.at[rows, :], sems.at[1, c])
        store.start()
        stores.append(store)
        g_out = dot_t0(act, grad_lifted)
        g_in = dot_t0(joined, gpre)
        sum_bias = sum_bias + jnp.sum(gpre.astype(F32), axis=0, keepdims=True)
        if c == 0:
            sum_in[...] = g_in
            sum_out[...] = g_out
        else:
            sum_in[...] += g_in
            sum_out[...] += g_out
    bias = jnp.concatenate([sum_bias[:, :HALF], sum_bias[:, HALF:], jnp.zeros((6, HALF), F32)], axis=0)
    mine = lax.axis_index("core")
    for half, out in ((mine, keep_ref), (1 - mine, give_ref)):
        for k in range(CHUNKS):
            top = sum_in[pl.ds(pl.multiple_of(32 * k + 16 * half, 8), 16), :]
            low = sum_out[pl.ds(pl.multiple_of(16 * k + 8 * half, 8), 8), :]
            last = bias if k == 0 else jnp.zeros((8, HALF), F32)
            piece = jnp.concatenate(
                [top[:, :HALF], low[:, :HALF], top[:, HALF:], low[:, HALF:], last], axis=0
            )
            out[k] = piece.astype(out.dtype)
    for store in stores:
        store.wait()


def back_kernel(
    src_ref, dst_ref, vals_ref, gpre_hbm, win_hbm, cot_hbm, own_hbm, o0, o1, o2, o3, o4, o5,
    gpre, win, cot, grad_agg, total, sems,
):
    loads = [
        pltpu.make_async_copy(win_hbm, win, sems.at[0]),
        pltpu.make_async_copy(gpre_hbm, gpre, sems.at[1]),
        pltpu.make_async_copy(cot_hbm, cot, sems.at[2]),
    ]
    for load in loads:
        load.start()
    total[pl.ds(NB, PEERS)] = jnp.zeros((PEERS, BLK, H), F32)
    for load in loads:
        load.wait()
    w_in = win[...]
    per = BACK // BLK
    for c in range(N // BACK):
        rows = pl.ds(c * BACK, BACK)
        joined = dot_t1(gpre[rows, :], w_in)
        grad_agg[rows, :] = joined[:, H:].astype(BF16)
        direct = cot[rows, :].astype(F32) + joined[:, :H]
        total[pl.ds(c * per, per)] = direct.reshape(per, BLK, H)

    def step(i, _):
        for u in range(BACK_STEP):
            t = i * BACK_STEP + u
            s, d = src_ref[t], dst_ref[t]
            down = grad_agg[pl.ds(pl.multiple_of(d * BLK, BLK), BLK), :]
            total[s] += dot_t0(vals_ref[t], down)
        return 0

    lax.fori_loop(0, T // BACK_STEP, step, 0)
    store = pltpu.make_async_copy(total.at[pl.ds(0, NB)], own_hbm, sems.at[3])
    store.start()
    me = lax.axis_index("sub")
    for d, o in enumerate((o0, o1, o2, o3, o4, o5)):
        q = lax.rem(me + d, SUB) if d < SUB else d
        o[...] = total[NB + q].astype(BF16)
    store.wait()


def land_kernel(
    rows_hbm, count_hbm, r0, r1, r2, r3, r4, r5, own_hbm, out_hbm, rows_ref, count, own, sems
):
    loads = [
        pltpu.make_async_copy(rows_hbm, rows_ref, sems.at[0]),
        pltpu.make_async_copy(count_hbm, count, sems.at[1]),
        pltpu.make_async_copy(own_hbm, own, sems.at[2]),
    ]
    for load in loads:
        load.start()
    for load in loads[:2]:
        load.wait()
    me = lax.axis_index("sub")
    lane = lax.broadcasted_iota(jnp.int32, (1, BLK), 1)
    ids = []
    for d in range(PEERS):
        q = lax.rem(me + SUB - d, SUB) if d < SUB else d
        ids.append(jnp.where(lane < count[0, q], rows_ref[q], -1))
    ids = jnp.concatenate(ids, axis=1)
    back = jnp.concatenate([r[...] for r in (r0, r1, r2, r3, r4, r5)], axis=0)
    stores = []
    for c in range(N // LAND):
        node = lax.broadcasted_iota(jnp.int32, (LAND, PEERS * BLK), 0) + c * LAND
        hot = jnp.where(node == ids, 1.0, 0.0).astype(BF16)
        landed = dot(hot, back)
        if c == 0:
            loads[2].wait()
        per = LAND // BLK
        blocks = pl.ds(c * per, per)
        own[blocks] += landed.reshape(per, BLK, H)
        store = pltpu.make_async_copy(own.at[blocks], out_hbm.at[blocks], sems.at[3 + c])
        store.start()
        stores.append(store)
    for store in stores:
        store.wait()


def join_kernel(keep, other, out_ref):
    out_ref[...] = (keep[...] + other[...].astype(F32)).astype(BF16)


def spread_kernel(parts, out_ref):
    whole = jnp.sum(parts[...].astype(F32), axis=0).astype(BF16)
    for i in range(out_ref.shape[0]):
        out_ref[i] = whole


def clip_kernel(keep, other, in_ref, bias_ref, out_ref):
    norms = []
    for part in (keep, other):
        squares = jnp.zeros((8, HALF), F32)
        for k in range(CHUNKS):
            piece = part[k].astype(F32)[:48]
            squares = squares + jnp.sum(jnp.square(piece).reshape(6, 8, HALF), axis=0)
        norms.append(jnp.sum(squares, keepdims=True))
    last = keep[0].astype(F32)[48:56]
    mine = lax.axis_index("core")
    last = jnp.where(mine == 0, last, other[0].astype(F32)[48:56])
    norm = norms[0] + norms[1] + jnp.sum(jnp.square(last), keepdims=True)
    factor = jnp.minimum(1.0, clip_norm * lax.rsqrt(norm + 1e-06))
    for half, part in ((mine, keep), (1 - mine, other)):
        for k in range(CHUNKS):
            piece = part[k].astype(F32) * factor
            top = jnp.concatenate([piece[0:16], piece[24:40]], axis=1)
            low = jnp.concatenate([piece[16:24], piece[40:48]], axis=1)
            in_ref[pl.ds(pl.multiple_of(32 * k + 16 * half, 8), 16), :] = top
            out_ref[pl.ds(pl.multiple_of(16 * k + 8 * half, 8), 8), :] = low
    bias_ref[...] = jnp.concatenate([last[0:1], last[1:2]], axis=1) * factor


def shift(value, axis, by, size):
    return lax.ppermute(value, axis, [(i, (i + by) % size) for i in range(size)])


def in_hbm(*values):
    return [pltpu.with_memory_space_constraint(v, pltpu.HBM) for v in values]


def exchange(slots):
    got = [slots[0]]
    got += [shift(slots[d], "sub", d, SUB) for d in range(1, SUB)]
    dom = 1
    for axis in DOM:
        dom *= lax.axis_size(axis)
    return got, dom


def local(feat, cot, vals, src, dst, halo_rows, halo_count, w_in, b_in, w_out):
    block = sds((BLK, H), BF16)
    halves = (CHUNKS, PROWS, HALF)
    by_slot = jnp.transpose(halo_rows, (1, 0, 2))
    slots = pl.pallas_call(
        pick_kernel,
        out_shape=[block] * PEERS,
        in_specs=[HB] * 3,
        out_specs=[VM] * PEERS,
        scratch_shapes=[
            pltpu.VMEM((PEERS, 1, BLK), jnp.int32),
            pltpu.SMEM((1, PEERS), jnp.int32),
            pltpu.VMEM((N, H), BF16),
            pltpu.VMEM((PEERS * BLK, N), BF16),
            pltpu.SemaphoreType.DMA((3,)),
        ],
        compiler_params=params(24),
        name="pick",
    )(*in_hbm(by_slot, halo_count, feat))
    got, dom = exchange(slots)
    got += [shift(slots[4], DOM, 1, dom), shift(slots[5], DOM, -1, dom)]
    near = pl.pallas_call(
        near_kernel,
        out_shape=sds((NB + 1, BLK, H), F32),
        in_specs=[HB] * 4,
        out_specs=VM,
        scratch_shapes=[
            pltpu.SMEM((T,), jnp.int32),
            pltpu.SMEM((T,), jnp.int32),
            pltpu.SMEM((T + NEAR_STEP,), jnp.int32),
            pltpu.VMEM((N, H), BF16),
            pltpu.VMEM((T, BLK, BLK), BF16),
            pltpu.SemaphoreType.DMA((4,)),
        ],
        compiler_params=params(24),
        cost_estimate=pl.CostEstimate(flops=800_000_000, bytes_accessed=6_000_000, transcendentals=0),
        name="near",
    )(*in_hbm(src, dst, feat, vals))
    new_rows, gpre, keep, give = pl.pallas_call(
        node_kernel,
        out_shape=[sds((N, H), BF16), pltpu.HBM((N, H), BF16), sds(halves, F32), sds(halves, BF16)],
        in_specs=[SM, SM] + [VM] * 13,
        out_specs=[HB] * 2 + [VM] * 2,
        scratch_shapes=[
            pltpu.SMEM((T + NEAR_STEP,), jnp.int32),
            pltpu.VMEM((PEERS, BLK, H), BF16),
            pltpu.VMEM((NB + 1, BLK, H), F32),
            pltpu.VMEM((2 * H, H), F32),
            pltpu.VMEM((H, H), F32),
            pltpu.VMEM((N, H), BF16),
            pltpu.VMEM((N, H), BF16),
            pltpu.SemaphoreType.DMA((2, N // CH)),
        ],
        compiler_params=params(32),
        name="node",
    )(src, dst, *got, feat, cot, vals, near, w_in, b_in.reshape(1, H), w_out)
    given = shift(give, "core", 1, 2)
    joined = pl.pallas_call(
        join_kernel, out_shape=sds(halves, BF16), in_specs=[VM] * 2, out_specs=VM, compiler_params=params(4), name="join"
    )(keep, given)
    parts = lax.all_to_all(joined, PLANE, split_axis=0, concat_axis=0, tiled=True)
    own, *slots = pl.pallas_call(
        back_kernel,
        out_shape=[pltpu.HBM((NB, BLK, H), F32)] + [block] * PEERS,
        in_specs=[SM, SM, VM] + [HB] * 3,
        out_specs=[HB] + [VM] * PEERS,
        scratch_shapes=[
            pltpu.VMEM((N, H), BF16),
            pltpu.VMEM((2 * H, H), BF16),
            pltpu.VMEM((N, H), BF16),
            pltpu.VMEM((N, H), BF16),
            pltpu.VMEM((BUF, BLK, H), F32),
            pltpu.SemaphoreType.DMA((4,)),
        ],
        compiler_params=params(20),
        cost_estimate=pl.CostEstimate(flops=4_000_000_000, bytes_accessed=9_000_000, transcendentals=0),
        name="back",
    )(src, dst, vals, *in_hbm(gpre, w_in, cot))
    parts, own = lax.optimization_barrier((parts, own))
    depth = lax.axis_size("z")
    paired = pl.pallas_call(
        spread_kernel,
        out_shape=sds((depth, PROWS, HALF), BF16),
        in_specs=[VM],
        out_specs=VM,
        compiler_params=params(4),
        name="fold",
    )(parts)
    paired, *slots[1:SUB] = lax.optimization_barrier((paired, *slots[1:SUB]))
    column = lax.all_to_all(paired, "z", split_axis=0, concat_axis=0, tiled=True)
    got = [slots[0]] + [shift(slots[d], "sub", d, SUB) for d in range(1, SUB)]
    spread = pl.pallas_call(
        spread_kernel,
        out_shape=sds(halves, BF16),
        in_specs=[VM],
        out_specs=VM,
        compiler_params=params(4),
        name="spread",
    )(column)
    spread, *far = lax.optimization_barrier((spread, *slots[SUB:]))
    whole = lax.all_to_all(spread, PLANE, split_axis=0, concat_axis=0, tiled=True)
    got += [shift(far[0], DOM, -1, dom), shift(far[1], DOM, 1, dom)]
    grad_features = pl.pallas_call(
        land_kernel,
        out_shape=sds((NB, BLK, H), F32),
        in_specs=[HB] * 2 + [VM] * PEERS + [HB],
        out_specs=HB,
        scratch_shapes=[
            pltpu.VMEM((PEERS, 1, BLK), jnp.int32),
            pltpu.SMEM((1, PEERS), jnp.int32),
            pltpu.VMEM((NB, BLK, H), F32),
            pltpu.SemaphoreType.DMA((3 + N // LAND,)),
        ],
        compiler_params=params(20),
        cost_estimate=pl.CostEstimate(flops=5_000_000_000, bytes_accessed=9_000_000, transcendentals=0),
        name="land",
    )(*in_hbm(by_slot, halo_count), *got, *in_hbm(own)).reshape(N, H)
    whole, grad_features = lax.optimization_barrier((whole, grad_features))
    other = shift(whole, "core", 1, 2)
    g_in, g_bias, g_out = pl.pallas_call(
        clip_kernel,
        out_shape=[sds((2 * H, H), F32), sds((1, H), F32), sds((H, H), F32)],
        in_specs=[VM] * 2,
        out_specs=[VM] * 3,
        compiler_params=params(8),
        name="clip",
    )(whole, other)
    return new_rows, grad_features, g_in, g_bias.reshape(H), g_out


def solution(mesh):
    grid = Mesh(mesh.devices.reshape(4, 8, 2, 4), ALL)
    split2, split1 = P(ALL, None), P(ALL)
    split3 = P(ALL, None, None)
    return jax.shard_map(
        local,
        mesh=grid,
        in_specs=(split2, split2, split3, split1, split1, split3, split2, P(), P(), P()),
        out_specs=(split2, split2, P(), P(), P()),
        check_vma=False,
    )
```
